32 devices in a mesh: seq: 8 (over z, y), rep: 4 (over x, core).
Axes of the slice: x: 2, y: 2, z: 4, core: 2. Of those that a mesh axis runs over, the one named last changes fastest.
Arguments:
- hidden: bfloat16 [2048, 4096], P('seq'), may hold values from -6 to 6
- seg_ids: int32 [2048], P('seq'), may hold values from 0 to 3, never falling along the last dimension, each value on 1 to 1024 neighbouring positions
- x_weight: bfloat16 [4096, 4096], P('seq', 'rep'), may hold values from -0.09375 to 0.09375
- bc_weight: bfloat16 [4096, 256], P('seq', 'rep'), may hold values from -0.02734375 to 0.02734375
- dt_weight: bfloat16 [4096, 32], P('seq', 'rep'), may hold values from -0.09375 to 0.09375
- dt_bias: float32 [32], P('rep'), may hold values from -3 to -1.5
- decay_rate: float32 [32], P('rep'), may hold values from 0.0001953125 to 0.5
- skip: float32 [32], P('rep'), may hold values from 0.5 to 1.5
Outputs:
- mixed: bfloat16 [2048, 4096], P('seq', 'rep')
The draws below stay inside these ranges and needn't reach their ends.
Inputs may be any that keep to these rules, and one draw needn't show every extreme that they name: `seg_ids`: ids never fall; each id covers 1 to 1024 consecutive tokens and some id covers exactly 1024.
All inputs are finite; a program needn't handle non-finite values.
Results may differ from the reference program's by a relative error of at most 0.007.
Values may be sent and summed in bfloat16 or wider, within the bound.
No kernel may reach another device: no remote copies, remote signals or barrier semaphores. Data moves between devices by JAX's collectives and lax.ppermute only.
A program may use at most 192 MiB of HBM per device.

```python
import math
import jax
import jax.numpy as jnp
import numpy as np
from jax import lax

D = 4096
H = 32
P_SIZE = 128
NS = 128
GROUP = 256
TOKENS = 2048
DOCS = 4
DOC_MAX = 1024


def steps_of(stream_key, dims, cuts, least, top_value):
    def one(axis_at, shards_of):
        steps = jax.random.uniform(jax.random.fold_in(jax.random.fold_in(stream_key, 6), axis_at), (shards_of,), jnp.float32, least / len(cuts), top_value / len(cuts))
        return jnp.repeat(jnp.exp(steps), dims[axis_at] // shards_of).reshape((-1,) + (1,) * (len(dims) - axis_at - 1))

    level = one(*cuts[0])
    for cut in cuts[1:]:
        level = level * one(*cut)
    return level


def split_up(number_of, total, bound, lean):
    loads = [(1 << 20) // math.isqrt(grade ** lean) + 1 for grade in range(2, number_of + 1)]
    surplus, counts = total - bound - (number_of - 1), [1] * (number_of - 1)
    while surplus > 0:
        movable = [i for i in range(number_of - 1) if counts[i] < bound]
        pool, remaining = sum([loads[i] for i in movable]), surplus
        for i in movable:
            addition = min(bound - counts[i], max(1, remaining * loads[i] // pool), surplus)
            counts[i] = counts[i] + addition
            surplus = surplus - addition
    return np.array([bound] + counts)


def ragged_sizes(stream_key, count, total, bound, lean):
    if count == 2:
        one = jax.random.randint(stream_key, (), max(1, total - bound), min(bound, total - 1) + 1)
        return jnp.stack([one, total - one])
    sizes = jnp.asarray(split_up(count, total, bound, lean), jnp.int32)
    pairs = (count - 1) // 2
    source_of, receiver = sizes[1:1 + 2 * pairs:2], sizes[2:2 + 2 * pairs:2]
    slack = jnp.minimum(source_of - 1, bound - receiver)
    passed = jax.random.randint(jax.random.fold_in(stream_key, 1), (pairs,), 0, 1 << 20) % (slack + 1)
    sizes = sizes.at[1:1 + 2 * pairs:2].set(source_of - passed).at[2:2 + 2 * pairs:2].set(receiver + passed)
    return sizes[jax.random.permutation(jax.random.fold_in(stream_key, 2), count)]


def bell_draw(rng, shape, deviation, limit, split=(), dtype=jnp.bfloat16):
    array = jax.random.normal(rng, shape, jnp.float32) * deviation
    if len(split) > 0:
        array = steps_of(rng, shape, split, -0.22, 0.18) * array
    return jnp.clip(array, min=-limit, max=limit).astype(dtype)


def setup_inputs(seed: int = 0) -> dict:
    key_of = jax.random.split(jax.random.key(seed), 9)
    return {
        "hidden": bell_draw(key_of[0], (TOKENS, D), 1.0, 6.0, ((0, 8),)),
        "seg_ids": jnp.searchsorted(jnp.cumsum(ragged_sizes(key_of[1], DOCS, TOKENS, DOC_MAX, 2)), jnp.arange(TOKENS), side="right").astype(jnp.int32),
        "x_weight": bell_draw(key_of[2], (D, H * P_SIZE), D ** -0.5, 0.09375, ((0, 8), (1, 4))),
        "bc_weight": bell_draw(key_of[3], (D, 2 * NS), (D * 12) ** -0.5, 0.02734375, ((0, 8), (1, 4))),
        "dt_weight": bell_draw(key_of[4], (D, H), D ** -0.5, 0.09375, ((0, 8), (1, 4))),
        "dt_bias": jnp.clip(-3.0 + 1.5 * jax.random.uniform(key_of[5], (H,), jnp.float32) ** steps_of(key_of[5], (H,), ((0, 4),), -0.2, 0.2), -3.0, -1.5),
        "decay_rate": jnp.clip(jnp.exp(math.log(0.5) - 7.8477625 * jax.random.uniform(key_of[6], (H,), jnp.float32) ** steps_of(key_of[6], (H,), ((0, 4),), -0.2, 0.2)), 0.0001953125, 0.5),
        "skip": jnp.clip(0.5 + 1.0 * jax.random.uniform(key_of[7], (H,), jnp.float32) ** steps_of(key_of[7], (H,), ((0, 4),), -0.2, 0.2), 0.5, 1.5),
    }


def state_read(c_block, state):
    upper_part = state.astype(jnp.bfloat16)
    lower_part = (state - upper_part.astype(jnp.float32)).astype(jnp.bfloat16)
    c_wide = c_block.astype(jnp.float32)
    first = jnp.einsum('tn,hnp->thp', c_wide, upper_part.astype(jnp.float32))
    second = jnp.einsum('tn,hnp->thp', c_wide, lower_part.astype(jnp.float32))
    return first + second


def block_step(state, prev_seg, x_block, b_block, c_block, dt_block, rate_block, seg_block):
    count = x_block.shape[0]
    cum = jnp.cumsum(rate_block, axis=0)
    order = jnp.arange(count)
    masked = (order[:, None] >= order[None, :]) & (seg_block[:, None] == seg_block[None, :])
    scores = jnp.dot(c_block, b_block.T, preferred_element_type=jnp.float32)
    cum_heads = cum.T
    gaps = cum_heads[:, :, None] - cum_heads[:, None, :]
    decay = jnp.where(masked[None], jnp.exp(jnp.where(masked[None], gaps, 0.0)), 0.0)
    mixing = (scores[None] * decay * dt_block.T[:, None, :]).astype(jnp.bfloat16)
    diag_part = jnp.einsum('htj,jhp->thp', mixing.astype(jnp.float32), x_block.astype(jnp.float32))
    keep = (seg_block == prev_seg).astype(jnp.float32)
    factor = jnp.exp(cum) * keep[:, None]
    carried = state_read(c_block, state) * factor[:, :, None]
    last_seg = seg_block[count - 1]
    tail = jnp.exp(cum[count - 1][None, :] - cum) * dt_block * (seg_block == last_seg).astype(jnp.float32)[:, None]
    loaded = (tail.T[:, :, None] * b_block.astype(jnp.float32)[None]).astype(jnp.bfloat16)
    built = jnp.einsum('hjn,jhp->hnp', loaded.astype(jnp.float32), x_block.astype(jnp.float32))
    through = jnp.exp(cum[count - 1]) * (last_seg == prev_seg).astype(jnp.float32)
    new_state = built + through[:, None, None] * state
    return diag_part + carried, new_state, last_seg


def reference(hidden, seg_ids, x_weight, bc_weight, dt_weight, dt_bias, decay_rate, skip):
    inputs = jnp.dot(hidden, x_weight, preferred_element_type=jnp.float32).astype(jnp.bfloat16)
    maps = jnp.dot(hidden, bc_weight, preferred_element_type=jnp.float32).astype(jnp.bfloat16)
    steps = jax.nn.softplus(jnp.dot(hidden, dt_weight, preferred_element_type=jnp.float32) + dt_bias)
    rates = -steps * decay_rate
    total = inputs.shape[0]
    blocks = total // GROUP
    x_all = inputs.reshape(blocks, GROUP, H, P_SIZE)
    b_all = maps[:, :NS].reshape(blocks, GROUP, NS)
    c_all = maps[:, NS:].reshape(blocks, GROUP, NS)
    dt_all = steps.reshape(blocks, GROUP, H)
    rate_all = rates.reshape(blocks, GROUP, H)
    seg_all = seg_ids.reshape(blocks, GROUP)

    def advance(carry, pieces):
        state, prev_seg = carry
        x_block, b_block, c_block, dt_block, rate_block, seg_block = pieces
        result, new_state, last_seg = block_step(state, prev_seg, x_block, b_block, c_block, dt_block, rate_block, seg_block)
        result = result + skip[None, :, None] * x_block.astype(jnp.float32)
        return (new_state, last_seg), result.astype(jnp.bfloat16).reshape(GROUP, H * P_SIZE)

    start = (jnp.zeros((H, NS, P_SIZE), jnp.float32), jnp.int32(-1))
    _, outputs = lax.scan(advance, start, (x_all, b_all, c_all, dt_all, rate_all, seg_all))
    return outputs.reshape(total, H * P_SIZE)
```

```python
import jax
import jax.numpy as jnp
from jax import lax
from jax.sharding import PartitionSpec as P

P_SIZE = 128
NS = 128
DOC_MAX = 1024
LANES = 2
PLANES = 4


def passed_along(x, axis, by):
    peers = lax.axis_size(axis)
    pairs = [(i, i + by) for i in range(peers) if 0 <= i + by < peers]
    return lax.ppermute(x, axis, pairs)


def state_read(c_block, state):
    upper_part = state.astype(jnp.bfloat16)
    lower_part = (state - upper_part.astype(jnp.float32)).astype(jnp.bfloat16)
    first = jnp.einsum("tn,hnp->thp", c_block, upper_part, preferred_element_type=jnp.float32)
    second = jnp.einsum("tn,hnp->thp", c_block, lower_part, preferred_element_type=jnp.float32)
    return first + second


def block_step(state, prev_seg, x_block, b_block, c_block, dt_block, rate_block, seg_block):
    count = x_block.shape[0]
    cum = jnp.cumsum(rate_block, axis=0)
    order = jnp.arange(count)
    masked = (order[:, None] >= order[None, :]) & (seg_block[:, None] == seg_block[None, :])
    scores = jnp.dot(c_block, b_block.T, preferred_element_type=jnp.float32)
    cum_heads = cum.T
    gaps = cum_heads[:, :, None] - cum_heads[:, None, :]
    decay = jnp.where(masked[None], jnp.exp(jnp.where(masked[None], gaps, 0.0)), 0.0)
    mixing = (scores[None] * decay * dt_block.T[:, None, :]).astype(jnp.bfloat16)
    diag_part = jnp.einsum("htj,jhp->thp", mixing, x_block, preferred_element_type=jnp.float32)
    keep = (seg_block == prev_seg).astype(jnp.float32)
    factor = jnp.exp(cum) * keep[:, None]
    carried = state_read(c_block, state) * factor[:, :, None]
    last_seg = seg_block[count - 1]
    tail = (
        jnp.exp(cum[count - 1][None, :] - cum)
        * dt_block
        * (seg_block == last_seg).astype(jnp.float32)[:, None]
    )
    loaded = (tail.T[:, :, None] * b_block.astype(jnp.float32)[None]).astype(jnp.bfloat16)
    built = jnp.einsum("hjn,jhp->hnp", loaded, x_block, preferred_element_type=jnp.float32)
    through = jnp.exp(cum[count - 1]) * (last_seg == prev_seg).astype(jnp.float32)
    new_state = built + through[:, None, None] * state
    return (diag_part + carried, new_state, last_seg)


def combine(earlier, later):
    early_state, early_keep, early_first, early_last = earlier
    late_state, late_keep, late_first, late_last = later
    linked = ((early_last == late_first) | (early_last < 0) | (late_first < 0)).astype(jnp.float32)
    passing = late_keep * linked
    return (
        late_state + passing[:, None, None] * early_state,
        early_keep * passing,
        jnp.where(early_first < 0, late_first, early_first),
        jnp.where(late_last < 0, early_last, late_last),
    )


def gathered_shards(hidden, seg_ids, x_weight, bc_weight, dt_weight, dt_bias, decay_rate, skip):
    tok_rows = hidden.shape[0]
    heads = dt_bias.shape[0]
    width = x_weight.shape[1]
    x_rows, bc_rows, dt_rows = (
        lax.all_gather(x_weight, "seq", axis=0, tiled=True),
        lax.all_gather(bc_weight, "seq", axis=0, tiled=True),
        lax.all_gather(dt_weight, "seq", axis=0, tiled=True),
    )
    x_total = jnp.dot(hidden, x_rows, preferred_element_type=jnp.float32)
    bc_total = jnp.dot(hidden, bc_rows, preferred_element_type=jnp.float32)
    dt_total = jnp.dot(hidden, dt_rows, preferred_element_type=jnp.float32)
    inputs = x_total.astype(jnp.bfloat16).reshape(tok_rows, heads, P_SIZE)
    maps = lax.all_gather(bc_total.astype(jnp.bfloat16), "rep", axis=1, tiled=True)
    b_all = maps[:, :NS]
    c_all = maps[:, NS:]
    steps = jax.nn.softplus(dt_total + dt_bias)
    rates = -steps * decay_rate
    state = jnp.zeros((heads, NS, P_SIZE), jnp.float32)
    prev_seg = jnp.int32(-1)
    result, state, prev_seg = block_step(
        state, prev_seg, inputs, b_all, c_all, steps, rates, seg_ids
    )
    whole_keep = jnp.exp(jnp.sum(rates, axis=0)) * (seg_ids[0] == seg_ids[tok_rows - 1]).astype(
        jnp.float32
    )
    element = (state, whole_keep, seg_ids[:1], seg_ids[tok_rows - 1 :])
    reach = DOC_MAX // tok_rows + 1
    first_hop = passed_along((element[0], element[1], element[2], element[3]), "seq", 1)
    incoming = first_hop
    for hop in range(reach - 1):
        incoming = combine(
            passed_along((incoming[0], incoming[1], incoming[2], incoming[3]), "seq", 1), first_hop
        )
    state_in = incoming[0]
    tag_in = incoming[3]
    running = jnp.cumsum(rates, axis=0)
    factor = jnp.exp(running) * (seg_ids == tag_in[0]).astype(jnp.float32)[:, None]
    extra = state_read(c_all, state_in) * factor[:, :, None]
    total_out = result + extra + skip[None, :, None] * inputs.astype(jnp.float32)
    return total_out.astype(jnp.bfloat16).reshape(tok_rows, width)


def pick(first, one, other):
    return jnp.where(first, one, other)


def split_hi_lo(value):
    upper = lax.reduce_precision(value, 8, 7)
    return upper.astype(jnp.bfloat16), (value - upper).astype(jnp.bfloat16)


def plane_shards(hidden, seg_ids, x_weight, bc_weight, dt_weight, dt_bias, decay_rate, skip):
    bf16, f32 = jnp.bfloat16, jnp.float32
    me = lax.axis_index("seq")
    lane, plane = me % LANES, me // LANES
    even = lane == 0
    core_even = lax.axis_index("rep") % 2 == 0
    rows, depth = hidden.shape
    k_rows, cols = x_weight.shape
    half = cols // 2
    heads = dt_bias.shape[0]
    mine_heads = heads // 2
    map_cols = bc_weight.shape[1]

    def at(p, l):
        return LANES * p + l

    swap = [(i, i ^ 1) for i in range(LANES * PLANES)]
    cores = [(i, i ^ 1) for i in range(lax.axis_size("rep"))]

    def shift(by, sources):
        return [(at(p, l), at(p + by, l)) for p in sources for l in range(LANES)]

    def ring(by):
        return [(at(p, l), at((p + by) % PLANES, l)) for p in range(PLANES) for l in range(LANES)]

    def send(x, pairs, axis="seq"):
        return lax.ppermute(x, axis, pairs)

    own = pick(even, x_weight[:, :half], x_weight[:, half:])
    other = send(pick(even, x_weight[:, half:], x_weight[:, :half]), swap)
    up_one = [send(w, shift(1, (0, 1, 2))) for w in (own, other)]
    down_one = [send(w, shift(-1, (1, 2, 3))) for w in (own, other)]

    small = jnp.concatenate([bc_weight, dt_weight], axis=1).T
    ids_row = jnp.pad(seg_ids.astype(bf16), (0, k_rows - rows))[None]
    used = map_cols + heads
    small = jnp.concatenate([small, ids_row, jnp.zeros((80 - used - 1, k_rows), bf16)], axis=0)
    from_ring = [small] + [send(small, ring(by)) for by in (3, 2, 1)]
    lane_small = jnp.stack(from_ring)
    lane_small = lax.dynamic_slice_in_dim(
        jnp.concatenate([lane_small, lane_small]), PLANES - plane, PLANES, 0
    )
    other_small = send(lane_small, swap)
    all_small = pick(
        even,
        jnp.stack([lane_small, other_small], 1),
        jnp.stack([other_small, lane_small], 1),
    )
    weights_small = all_small[:, :, :used].transpose(2, 0, 1, 3).reshape(used, depth)
    ids = all_small[:, :, used, :rows].astype(jnp.int32)
    totals = lax.dot_general(
        hidden, weights_small, (((1,), (1,)), ((), ())), preferred_element_type=f32
    )
    dt_hi, dt_lo = split_hi_lo(totals[:, map_cols:])
    pack = jnp.concatenate([totals[:, :map_cols].astype(bf16), dt_hi, dt_lo], axis=1)
    pack_other = send(pack, swap)
    both = pick(even, jnp.stack([pack, pack_other]), jnp.stack([pack_other, pack]))
    maps = lax.all_gather(both[:, :, :map_cols], "rep", axis=2, tiled=True)
    b_all, c_all = maps[:, :, :NS], maps[:, :, NS:]
    dt_total = both[:, :, map_cols : map_cols + heads].astype(f32) + both[
        :, :, map_cols + heads :
    ].astype(f32)

    def my_heads(x):
        return pick(even, x[..., :mine_heads], x[..., mine_heads:])

    steps = jax.nn.softplus(my_heads(dt_total) + my_heads(dt_bias))
    rates = -steps * my_heads(decay_rate)
    cum = jnp.cumsum(rates, axis=1)
    seg = lax.dynamic_index_in_dim(ids, plane, 0, keepdims=False)
    order = jnp.arange(rows)
    masked = (order[None, :, None] >= order[None, None, :]) & (seg[:, :, None] == seg[:, None, :])
    cum_heads = cum.transpose(0, 2, 1)
    gaps = cum_heads[:, :, :, None] - cum_heads[:, :, None, :]
    masked = masked[:, None]
    decay = jnp.where(masked, jnp.exp(jnp.where(masked, gaps, 0.0)), 0.0)
    scores = jnp.einsum("btn,bjn->btj", c_all, b_all, preferred_element_type=f32)
    mixing = (scores[:, None] * decay * steps.transpose(0, 2, 1)[:, :, None, :]).astype(bf16)
    last = seg[:, rows - 1]
    end = cum[:, rows - 1]
    tail = jnp.exp(end[:, None] - cum) * steps * (seg == last[:, None]).astype(f32)[:, :, None]
    loaded = (tail[..., None] * b_all.astype(f32)[:, :, None]).astype(bf16)
    link = jnp.exp(end[1]) * (last[1] == last[0]).astype(f32)
    through_plane = jnp.exp(end[0] + end[1])
    earlier_through = send(through_plane, shift(1, (0, 1, 2)))
    ends = ids[:, LANES - 1, rows - 1]
    tag = jnp.where(plane > 0, ends[jnp.maximum(plane - 1, 0)], -1)
    tag_before = jnp.where(plane > 1, ends[jnp.maximum(plane - 2, 0)], -1)
    earlier_link = earlier_through * (tag == tag_before).astype(f32)
    enters = jnp.exp(end[0]) * (last[0] == tag).astype(f32)
    factor0 = jnp.exp(cum[0]) * (seg[0] == tag).astype(f32)[:, None]
    factor1 = jnp.exp(cum[1]) * (seg[1] == last[0]).astype(f32)[:, None]

    near = send(pick(core_even, hidden[:, : depth // 2], hidden[:, depth // 2 :]), swap)
    far = send(near, cores, "rep")
    partner = pick(
        core_even,
        jnp.concatenate([near, far], axis=1),
        jnp.concatenate([far, near], axis=1),
    )
    tokens = pick(
        even,
        jnp.concatenate([hidden, partner], axis=0),
        jnp.concatenate([partner, hidden], axis=0),
    )

    def part(at_plane, weights):
        total = None
        for l, w in zip((lane, 1 - lane), weights):
            block = lax.dynamic_slice_in_dim(tokens, (LANES * at_plane + l) * k_rows, k_rows, 1)
            product = jnp.dot(block, w, preferred_element_type=f32)
            total = product if total is None else total + product
        return total

    up_two = [send(w, shift(1, (1, 2))) for w in up_one]
    down_two = [send(w, shift(-1, (1, 2))) for w in down_one]
    two = [a + b for a, b in zip(up_two, down_two)]
    three = [send(w, shift(1, (2,)) + shift(-1, (1,))) for w in two]
    x_total = part(plane, (own, other))
    x_total = x_total + part(jnp.maximum(plane - 1, 0), up_one)
    x_total = x_total + part(jnp.minimum(plane + 1, PLANES - 1), down_one)
    x_total = x_total + part((plane + 2) % PLANES, two)
    x_total = x_total + part(jnp.where(plane == 0, PLANES - 1, 0), three)
    inputs = x_total.astype(bf16).reshape(LANES, rows, mine_heads, P_SIZE)

    built = jnp.einsum("bjhn,bjhp->bhnp", loaded, inputs, preferred_element_type=f32)
    ready = (built[1] + link[:, None, None] * built[0]).astype(bf16)
    from_one = send(ready, shift(1, (0, 1, 2)))
    from_two = send(ready, shift(2, (0, 1)))
    diag = jnp.einsum("bhtj,bjhp->bthp", mixing, inputs, preferred_element_type=f32)
    local = diag + my_heads(skip)[None, None, :, None] * inputs.astype(f32)
    carried = jnp.einsum("tn,hnp->thp", c_all[1], built[0].astype(bf16), preferred_element_type=f32)
    incoming = from_one.astype(f32) + earlier_link[:, None, None] * from_two.astype(f32)
    entering = incoming.astype(bf16)
    carry0 = jnp.einsum("tn,hnp->thp", c_all[0], entering, preferred_element_type=f32)
    carry1 = jnp.einsum("tn,hnp->thp", c_all[1], entering, preferred_element_type=f32)
    out0 = local[0] + factor0[:, :, None] * carry0
    out1 = local[1] + factor1[:, :, None] * (carried + enters[None, :, None] * carry1)
    out0 = out0.astype(bf16).reshape(rows, half)
    out1 = out1.astype(bf16).reshape(rows, half)
    swapped = send(pick(even, out1, out0), swap)
    kept = pick(even, out0, out1)
    return pick(
        even,
        jnp.concatenate([kept, swapped], axis=1),
        jnp.concatenate([swapped, kept], axis=1),
    )


def solution(mesh):
    placed = (
        P("seq", None),
        P("seq"),
        P("seq", "rep"),
        P("seq", "rep"),
        P("seq", "rep"),
        P("rep"),
        P("rep"),
        P("rep"),
    )
    by_planes = mesh.shape["seq"] == LANES * PLANES and mesh.shape["rep"] % 2 == 0
    return jax.shard_map(
        plane_shards if by_planes else gathered_shards,
        mesh=mesh,
        in_specs=placed,
        out_specs=P("seq", "rep"),
        check_vma=False,
    )
```

```python
import functools
import math

import jax
import jax.numpy as jnp
from jax import lax
from jax.experimental import pallas as pl
from jax.experimental.pallas import tpu as pltpu
from jax.sharding import PartitionSpec as P

P_SIZE = 128
NS = 128
DOC_MAX = 1024
LANES = 2
PLANES = 4


def passed_along(x, axis, by):
    peers = lax.axis_size(axis)
    pairs = [(i, i + by) for i in range(peers) if 0 <= i + by < peers]
    return lax.ppermute(x, axis, pairs)


def state_read(c_block, state):
    upper_part = state.astype(jnp.bfloat16)
    lower_part = (state - upper_part.astype(jnp.float32)).astype(jnp.bfloat16)
    first = jnp.einsum("tn,hnp->thp", c_block, upper_part, preferred_element_type=jnp.float32)
    second = jnp.einsum("tn,hnp->thp", c_block, lower_part, preferred_element_type=jnp.float32)
    return first + second


def block_step(state, prev_seg, x_block, b_block, c_block, dt_block, rate_block, seg_block):
    count = x_block.shape[0]
    cum = jnp.cumsum(rate_block, axis=0)
    order = jnp.arange(count)
    masked = (order[:, None] >= order[None, :]) & (seg_block[:, None] == seg_block[None, :])
    scores = jnp.dot(c_block, b_block.T, preferred_element_type=jnp.float32)
    cum_heads = cum.T
    gaps = cum_heads[:, :, None] - cum_heads[:, None, :]
    decay = jnp.where(masked[None], jnp.exp(jnp.where(masked[None], gaps, 0.0)), 0.0)
    mixing = (scores[None] * decay * dt_block.T[:, None, :]).astype(jnp.bfloat16)
    diag_part = jnp.einsum("htj,jhp->thp", mixing, x_block, preferred_element_type=jnp.float32)
    keep = (seg_block == prev_seg).astype(jnp.float32)
    factor = jnp.exp(cum) * keep[:, None]
    carried = state_read(c_block, state) * factor[:, :, None]
    last_seg = seg_block[count - 1]
    tail = (
        jnp.exp(cum[count - 1][None, :] - cum)
        * dt_block
        * (seg_block == last_seg).astype(jnp.float32)[:, None]
    )
    loaded = (tail.T[:, :, None] * b_block.astype(jnp.float32)[None]).astype(jnp.bfloat16)
    built = jnp.einsum("hjn,jhp->hnp", loaded, x_block, preferred_element_type=jnp.float32)
    through = jnp.exp(cum[count - 1]) * (last_seg == prev_seg).astype(jnp.float32)
    new_state = built + through[:, None, None] * state
    return (diag_part + carried, new_state, last_seg)


def combine(earlier, later):
    early_state, early_keep, early_first, early_last = earlier
    late_state, late_keep, late_first, late_last = later
    linked = ((early_last == late_first) | (early_last < 0) | (late_first < 0)).astype(jnp.float32)
    passing = late_keep * linked
    return (
        late_state + passing[:, None, None] * early_state,
        early_keep * passing,
        jnp.where(early_first < 0, late_first, early_first),
        jnp.where(late_last < 0, early_last, late_last),
    )


def gathered_shards(hidden, seg_ids, x_weight, bc_weight, dt_weight, dt_bias, decay_rate, skip):
    tok_rows = hidden.shape[0]
    heads = dt_bias.shape[0]
    width = x_weight.shape[1]
    x_rows, bc_rows, dt_rows = (
        lax.all_gather(x_weight, "seq", axis=0, tiled=True),
        lax.all_gather(bc_weight, "seq", axis=0, tiled=True),
        lax.all_gather(dt_weight, "seq", axis=0, tiled=True),
    )
    x_total = jnp.dot(hidden, x_rows, preferred_element_type=jnp.float32)
    bc_total = jnp.dot(hidden, bc_rows, preferred_element_type=jnp.float32)
    dt_total = jnp.dot(hidden, dt_rows, preferred_element_type=jnp.float32)
    inputs = x_total.astype(jnp.bfloat16).reshape(tok_rows, heads, P_SIZE)
    maps = lax.all_gather(bc_total.astype(jnp.bfloat16), "rep", axis=1, tiled=True)
    b_all = maps[:, :NS]
    c_all = maps[:, NS:]
    steps = jax.nn.softplus(dt_total + dt_bias)
    rates = -steps * decay_rate
    state = jnp.zeros((heads, NS, P_SIZE), jnp.float32)
    prev_seg = jnp.int32(-1)
    result, state, prev_seg = block_step(
        state, prev_seg, inputs, b_all, c_all, steps, rates, seg_ids
    )
    whole_keep = jnp.exp(jnp.sum(rates, axis=0)) * (seg_ids[0] == seg_ids[tok_rows - 1]).astype(
        jnp.float32
    )
    element = (state, whole_keep, seg_ids[:1], seg_ids[tok_rows - 1 :])
    reach = DOC_MAX // tok_rows + 1
    first_hop = passed_along((element[0], element[1], element[2], element[3]), "seq", 1)
    incoming = first_hop
    for hop in range(reach - 1):
        incoming = combine(
            passed_along((incoming[0], incoming[1], incoming[2], incoming[3]), "seq", 1), first_hop
        )
    state_in = incoming[0]
    tag_in = incoming[3]
    running = jnp.cumsum(rates, axis=0)
    factor = jnp.exp(running) * (seg_ids == tag_in[0]).astype(jnp.float32)[:, None]
    extra = state_read(c_all, state_in) * factor[:, :, None]
    total_out = result + extra + skip[None, :, None] * inputs.astype(jnp.float32)
    return total_out.astype(jnp.bfloat16).reshape(tok_rows, width)


def pick(first, one, other):
    return jnp.where(first, one, other)


def after(x, *earlier):
    return lax.optimization_barrier((x, *earlier))[0]


def call(body, outs, *operands, flops=0, scratch=()):
    single = not isinstance(outs, list)
    shapes = [outs] if single else outs
    size = sum(math.prod(o.shape) * o.dtype.itemsize for o in (*operands, *shapes))
    result = pl.pallas_call(
        body,
        out_shape=shapes,
        in_specs=[pl.BlockSpec(memory_space=pltpu.SMEM)]
        + [pl.BlockSpec(memory_space=pltpu.VMEM)] * (len(operands) - 1),
        out_specs=[pl.BlockSpec(memory_space=pltpu.VMEM)] * len(shapes),
        scratch_shapes=list(scratch),
        compiler_params=pltpu.CompilerParams(vmem_limit_bytes=40 * 2**20),
        cost_estimate=pl.CostEstimate(flops=flops, bytes_accessed=size, transcendentals=0),
    )(*operands)
    return result[0] if single else result


def contract_last(a, b):
    return lax.dot_general(a, b, (((1,), (1,)), ((), ())), preferred_element_type=jnp.float32)


def mul(a, b):
    return jnp.dot(a, b, preferred_element_type=jnp.float32)


def depth_blocks(place, token_refs, at, size):
    hidden_ref, near_ref, far_ref = token_refs
    own = hidden_ref[:, pl.ds(pl.multiple_of(at * size, size), size)]
    blocks = near_ref.shape[1] // size
    inside = pl.ds(pl.multiple_of((at % blocks) * size, size), size)
    is_near = (at // blocks) == place[2]
    return own, jnp.where(is_near, near_ref[:, inside], far_ref[:, inside])


def share_kernel(used, place, hidden, near, far, s0, s1, s2, s3, out):
    plane, lane = place[0], place[1]
    rows = hidden.shape[0]
    size = s0.shape[1]
    totals = [None, None]
    for back, s in enumerate((s0, s1, s2, s3)):
        at = LANES * ((plane + PLANES - back) % PLANES) + lane
        weights = s[...]
        for r, tokens in enumerate(depth_blocks(place, (hidden, near, far), at, size)):
            product = contract_last(weights, tokens)
            totals[r] = product if totals[r] is None else totals[r] + product
    row = lax.broadcasted_iota(jnp.int32, (s0.shape[0] - used, rows), 0)
    ids = s0[used:, :rows].astype(jnp.float32)
    ends = [s[used:, :rows].astype(jnp.float32)[0:1, rows - 1 : rows] for s in (s1, s2)]
    notes = jnp.where(row == 1, ends[0], jnp.where(row == 2, ends[1], ids))
    out[:used, :rows] = totals[0][:used]
    out[:used, rows:] = totals[1][:used]
    out[used:, :rows] = notes
    out[used:, rows:] = jnp.zeros_like(notes)


def decay_kernel(
    map_cols, place, maps, total, bias, rate_of, mixing, loaded, c_out, fac, meta
):
    f32, bf16 = jnp.float32, jnp.bfloat16
    plane, lane = place[0], place[1]
    heads = bias.shape[0]
    mine = heads // 2
    rows = total.shape[1] // 2
    even = lane == 0
    pre = total[map_cols : map_cols + heads, :] + bias[...]
    steps = jnp.maximum(pre, 0.0) + jnp.log1p(jnp.exp(-jnp.abs(pre)))
    rates = -steps * rate_of[...]
    steps = jnp.where(even, steps[:mine], steps[mine:])
    rates = jnp.where(even, rates[:mine], rates[mine:])
    notes = total[map_cols + heads :, :]
    tri_row = lax.broadcasted_iota(jnp.int32, (rows, rows), 0)
    tri_col = lax.broadcasted_iota(jnp.int32, (rows, rows), 1)
    upper = (tri_row <= tri_col).astype(f32)
    causal = tri_row >= tri_col
    pad = jnp.zeros((8 - mine, rows), f32)
    cums, lasts = [], []
    for r in range(2):
        cut = slice(r * rows, (r + 1) * rows)
        cums.append(
            lax.dot_general(
                jnp.concatenate([rates[:, cut], pad], axis=0),
                upper,
                (((1,), (0,)), ((), ())),
                precision=lax.Precision.HIGHEST,
                preferred_element_type=f32,
            )
        )
        lasts.append(notes[0:1, (r + 1) * rows - 1 : (r + 1) * rows])
    end = [c[:mine, rows - 1 : rows] for c in cums]
    end0, end1 = pick(even, end[0], end[1]), pick(even, end[1], end[0])
    last0, last1 = pick(even, lasts[0], lasts[1]), pick(even, lasts[1], lasts[0])
    final = pick(even, notes[:, 2 * rows - 1 :], notes[:, rows - 1 : rows])
    tag = jnp.where(plane > 0, final[1:2], -1.0)
    tag_before = jnp.where(plane > 1, final[2:3], -1.0)
    link = jnp.exp(end1) * (last1 == last0).astype(f32)
    enters = jnp.exp(end0) * (last0 == tag).astype(f32)
    through = jnp.exp(end0 + end1)
    passes = (tag == tag_before).astype(f32)
    width = meta.shape[1] // mine
    meta[...] = jnp.zeros_like(meta)
    for h in range(mine):
        cut = slice(h * width, (h + 1) * width)
        meta[0:1, cut] = jnp.broadcast_to(link[h : h + 1], (1, width))
        meta[1:2, cut] = jnp.broadcast_to(enters[h : h + 1], (1, width))
        meta[2:3, cut] = jnp.broadcast_to(through[h : h + 1], (1, width))
        meta[3:4, cut] = jnp.broadcast_to(passes, (1, width))
    for r in range(2):
        b = lane if r == 0 else 1 - lane
        cut = slice(r * rows, (r + 1) * rows)
        seg, cum, dt = notes[0:1, cut], cums[r], steps[:, cut]
        source = jnp.where(b == 0, tag, last0)
        factor = jnp.exp(cum) * (seg == source).astype(f32)
        fac[b] = factor.T
        cols = jnp.concatenate([cum[:mine], jnp.broadcast_to(seg, (8 - mine, rows))], axis=0).T
        keep = causal & (cols[:, mine : mine + 1] == seg)
        b_t, c_t = maps[:NS, cut], maps[NS:, cut]
        c_rows = c_t.astype(f32).T.astype(bf16)
        c_out[b] = c_rows
        scores = mul(c_rows, b_t)
        tail = jnp.exp(end[r] - cum[:mine]) * dt * (seg == lasts[r]).astype(f32)
        wide = b_t.astype(f32)
        for h in range(mine):
            gap = cols[:, h : h + 1] - cum[h : h + 1]
            decay = jnp.where(keep, jnp.exp(jnp.where(keep, gap, 0.0)), 0.0)
            mixing[b, h] = (scores * decay * dt[h : h + 1]).astype(bf16)
            loaded[b, h] = (wide * tail[h : h + 1]).astype(bf16)


def early_kernel(place, hidden, near, far, own, other, uo, up, do, dp, two, out):
    plane, lane = place[0], place[1]
    size = own.shape[0]
    sources = (
        (plane, own, other),
        (jnp.maximum(plane - 1, 0), uo, up),
        (jnp.minimum(plane + 1, PLANES - 1), do, dp),
        ((plane + 2) % PLANES, two.at[:size], two.at[size:]),
    )
    totals = [None, None]
    for at_plane, w_lane, w_other in sources:
        for l, w in ((lane, w_lane), (1 - lane, w_other)):
            weights = w[...]
            blocks = depth_blocks(place, (hidden, near, far), LANES * at_plane + l, size)
            for r, tokens in enumerate(blocks):
                product = mul(tokens, weights)
                totals[r] = product if totals[r] is None else totals[r] + product
    out[0] = totals[0]
    out[1] = totals[1]


def input_kernel(place, hidden, near, far, acc, three, loaded, meta, x_out, ready, built_out):
    f32, bf16 = jnp.float32, jnp.bfloat16
    plane, lane = place[0], place[1]
    size = three.shape[0] // 2
    at_plane = jnp.where(plane == 0, PLANES - 1, 0)
    totals = [acc[0], acc[1]]
    for l, w in ((lane, three.at[:size]), (1 - lane, three.at[size:])):
        weights = w[...]
        blocks = depth_blocks(place, (hidden, near, far), LANES * at_plane + l, size)
        for r, tokens in enumerate(blocks):
            totals[r] = totals[r] + mul(tokens, weights)
    x_out[lane] = totals[0].astype(bf16)
    x_out[1 - lane] = totals[1].astype(bf16)
    mine = loaded.shape[1]
    width = meta.shape[1] // mine
    for h in range(mine):
        cut = slice(h * width, (h + 1) * width)
        first = mul(loaded[0, h], x_out[0, :, cut])
        second = mul(loaded[1, h], x_out[1, :, cut])
        ready[:NS, cut] = (second + meta[0:1, cut] * first).astype(bf16)
        built_out[:, cut] = first.astype(bf16)
    through = meta[2:3, :]
    upper = through.astype(bf16)
    lower = (through - upper.astype(f32)).astype(bf16)
    row = lax.broadcasted_iota(jnp.int32, (ready.shape[0] - NS, ready.shape[1]), 0)
    ready[NS:, :] = jnp.where(
        row == 0, upper.astype(f32), jnp.where(row == 1, lower.astype(f32), 0.0)
    ).astype(bf16)


def local_kernel(place, x, mixing, skip, c_rows, built, fac, out):
    lane = place[1]
    mine = mixing.shape[1]
    width = x.shape[2] // mine
    carried = mul(c_rows[1], built[...])
    gains = jnp.where(lane == 0, skip[:, :mine], skip[:, mine:])
    for h in range(mine):
        cut = slice(h * width, (h + 1) * width)
        for b in range(2):
            xs = x[b, :, cut]
            local = mul(mixing[b, h], xs) + gains[:, h : h + 1] * xs.astype(jnp.float32)
            if b == 1:
                local = local + fac[1, :, h : h + 1] * carried[:, cut]
            out[b, :, cut] = local


def final_kernel(partner, mine, place, local, c_rows, fac, meta, one, two, out):
    f32, bf16 = jnp.float32, jnp.bfloat16
    lane = place[1]
    b = 1 - lane if partner else lane
    through = one[NS : NS + 1, :].astype(f32) + one[NS + 1 : NS + 2, :].astype(f32)
    incoming = one[:NS, :].astype(f32) + (through * meta[3:4, :]) * two[:NS, :].astype(f32)
    entering = (incoming * jnp.where(b == 1, meta[1:2, :], 1.0)).astype(bf16)
    carried = mul(c_rows[b], entering)
    factor = fac[b]
    width = out.shape[1] // mine
    for h in range(mine):
        cut = slice(h * width, (h + 1) * width)
        out[:, cut] = (local[b, :, cut] + factor[:, h : h + 1] * carried[:, cut]).astype(bf16)


def plane_shards(hidden, seg_ids, x_weight, bc_weight, dt_weight, dt_bias, decay_rate, skip):
    bf16, f32 = jnp.bfloat16, jnp.float32
    me = lax.axis_index("seq")
    lane, plane = me % LANES, me // LANES
    even = lane == 0
    core = lax.axis_index("rep") % 2
    place = jnp.stack([plane, lane, core]).astype(jnp.int32)
    rows, depth = hidden.shape
    k_rows, cols = x_weight.shape
    half = cols // 2
    heads = dt_bias.shape[0]
    mine = heads // 2
    map_cols = bc_weight.shape[1]
    used = map_cols + heads

    def shaped(dtype, *shape):
        return jax.ShapeDtypeStruct(shape, dtype)

    def at(p, l):
        return LANES * p + l

    swap = [(i, i ^ 1) for i in range(LANES * PLANES)]
    cores = [(i, i ^ 1) for i in range(lax.axis_size("rep"))]

    def shift(by, sources):
        return [(at(p, l), at(p + by, l)) for p in sources for l in range(LANES)]

    def ring(by):
        return [(at(p, l), at((p + by) % PLANES, l)) for p in range(PLANES) for l in range(LANES)]

    def send(x, pairs, axis="seq"):
        return lax.ppermute(x, axis, pairs)

    own = pick(even, x_weight[:, :half], x_weight[:, half:])
    other = send(pick(even, x_weight[:, half:], x_weight[:, :half]), swap)
    up_own, down_own = send(own, shift(1, (0, 1, 2))), send(own, shift(-1, (1, 2, 3)))
    up_other, down_other = send(other, shift(1, (0, 1, 2))), send(other, shift(-1, (1, 2, 3)))
    up_two = send(jnp.concatenate([up_own, up_other]), shift(1, (1, 2)))
    down_two = send(jnp.concatenate([down_own, down_other]), shift(-1, (1, 2)))
    two = up_two + down_two
    three = send(two, shift(1, (2,)) + shift(-1, (1,)))

    near = pick(core == 0, hidden[:, : depth // 2], hidden[:, depth // 2 :])
    near = send(after(near, other), swap)
    far = send(near, cores, "rep")

    ids_row = jnp.pad(seg_ids.astype(bf16), (0, k_rows - rows))[None]
    small = jnp.concatenate(
        [bc_weight.T, dt_weight.T, ids_row, jnp.zeros((7, k_rows), bf16)], axis=0
    )
    from_ring = [small] + [send(small, ring(by)) for by in (1, 2, 3)]
    share = call(
        functools.partial(share_kernel, used),
        shaped(f32, used + 8, LANES * rows),
        place,
        hidden,
        near,
        far,
        *from_ring,
        flops=4 * rows * depth * used,
    )
    share_other = send(share, swap)
    total = share + jnp.concatenate([share_other[:, rows:], share_other[:, :rows]], axis=1)
    maps = lax.all_gather(total[:map_cols].astype(bf16), "rep", axis=0, tiled=True)
    mixing, loaded, c_rows, fac, meta = call(
        functools.partial(decay_kernel, map_cols),
        [
            shaped(bf16, LANES, mine, rows, rows),
            shaped(bf16, LANES, mine, NS, rows),
            shaped(bf16, LANES, rows, NS),
            shaped(f32, LANES, rows, 8),
            shaped(f32, 8, half),
        ],
        place,
        maps,
        total,
        dt_bias[:, None],
        decay_rate[:, None],
        flops=100 * mine * rows * rows,
    )
    early = call(
        early_kernel,
        shaped(f32, LANES, rows, half),
        place,
        hidden,
        near,
        far,
        own,
        other,
        up_own,
        up_other,
        down_own,
        down_other,
        two,
        flops=4 * rows * depth * half,
    )
    inputs, ready, built = call(
        input_kernel,
        [
            shaped(bf16, LANES, rows, half),
            shaped(bf16, NS + 16, half),
            shaped(bf16, NS, half),
        ],
        place,
        hidden,
        near,
        far,
        early,
        three,
        loaded,
        meta,
        flops=rows * depth * half,
    )
    from_one = send(ready, shift(1, (0, 1, 2)))
    from_two = send(ready, shift(2, (0, 1)))
    local = call(
        local_kernel,
        shaped(f32, LANES, rows, half),
        place,
        inputs,
        mixing,
        skip[None],
        c_rows,
        built,
        fac,
        flops=4 * rows * rows * half,
    )

    def finish(partner):
        return call(
            functools.partial(final_kernel, partner, mine),
            shaped(bf16, rows, half),
            place,
            local,
            c_rows,
            fac,
            meta,
            from_one,
            from_two,
            flops=2 * rows * NS * half,
        )

    swapped = send(finish(True), swap)
    kept = finish(False)
    return pick(
        even,
        jnp.concatenate([kept, swapped], axis=1),
        jnp.concatenate([swapped, kept], axis=1),
    )


def solution(mesh):
    placed = (
        P("seq", None),
        P("seq"),
        P("seq", "rep"),
        P("seq", "rep"),
        P("seq", "rep"),
        P("rep"),
        P("rep"),
        P("rep"),
    )
    by_planes = mesh.shape["seq"] == LANES * PLANES and mesh.shape["rep"] % 2 == 0
    return jax.shard_map(
        plane_shards if by_planes else gathered_shards,
        mesh=mesh,
        in_specs=placed,
        out_specs=P("seq", "rep"),
        check_vma=False,
    )
```

```python
import functools
import math

import jax
import jax.numpy as jnp
from jax import lax
from jax.experimental import pallas as pl
from jax.experimental.pallas import tpu as pltpu
from jax.sharding import PartitionSpec as P

P_SIZE = 128
NS = 128
DOC_MAX = 1024
LANES = 2
PLANES = 4


def passed_along(x, axis, by):
    peers = lax.axis_size(axis)
    pairs = [(i, i + by) for i in range(peers) if 0 <= i + by < peers]
    return lax.ppermute(x, axis, pairs)


def state_read(c_block, state):
    upper_part = state.astype(jnp.bfloat16)
    lower_part = (state - upper_part.astype(jnp.float32)).astype(jnp.bfloat16)
    first = jnp.einsum("tn,hnp->thp", c_block, upper_part, preferred_element_type=jnp.float32)
    second = jnp.einsum("tn,hnp->thp", c_block, lower_part, preferred_element_type=jnp.float32)
    return first + second


def block_step(state, prev_seg, x_block, b_block, c_block, dt_block, rate_block, seg_block):
    count = x_block.shape[0]
    cum = jnp.cumsum(rate_block, axis=0)
    order = jnp.arange(count)
    masked = (order[:, None] >= order[None, :]) & (seg_block[:, None] == seg_block[None, :])
    scores = jnp.dot(c_block, b_block.T, preferred_element_type=jnp.float32)
    cum_heads = cum.T
    gaps = cum_heads[:, :, None] - cum_heads[:, None, :]
    decay = jnp.where(masked[None], jnp.exp(jnp.where(masked[None], gaps, 0.0)), 0.0)
    mixing = (scores[None] * decay * dt_block.T[:, None, :]).astype(jnp.bfloat16)
    diag_part = jnp.einsum("htj,jhp->thp", mixing, x_block, preferred_element_type=jnp.float32)
    keep = (seg_block == prev_seg).astype(jnp.float32)
    factor = jnp.exp(cum) * keep[:, None]
    carried = state_read(c_block, state) * factor[:, :, None]
    last_seg = seg_block[count - 1]
    tail = (
        jnp.exp(cum[count - 1][None, :] - cum)
        * dt_block
        * (seg_block == last_seg).astype(jnp.float32)[:, None]
    )
    loaded = (tail.T[:, :, None] * b_block.astype(jnp.float32)[None]).astype(jnp.bfloat16)
    built = jnp.einsum("hjn,jhp->hnp", loaded, x_block, preferred_element_type=jnp.float32)
    through = jnp.exp(cum[count - 1]) * (last_seg == prev_seg).astype(jnp.float32)
    new_state = built + through[:, None, None] * state
    return (diag_part + carried, new_state, last_seg)


def combine(earlier, later):
    early_state, early_keep, early_first, early_last = earlier
    late_state, late_keep, late_first, late_last = later
    linked = ((early_last == late_first) | (early_last < 0) | (late_first < 0)).astype(jnp.float32)
    passing = late_keep * linked
    return (
        late_state + passing[:, None, None] * early_state,
        early_keep * passing,
        jnp.where(early_first < 0, late_first, early_first),
        jnp.where(late_last < 0, early_last, late_last),
    )


def gathered_shards(hidden, seg_ids, x_weight, bc_weight, dt_weight, dt_bias, decay_rate, skip):
    tok_rows = hidden.shape[0]
    heads = dt_bias.shape[0]
    width = x_weight.shape[1]
    x_rows, bc_rows, dt_rows = (
        lax.all_gather(x_weight, "seq", axis=0, tiled=True),
        lax.all_gather(bc_weight, "seq", axis=0, tiled=True),
        lax.all_gather(dt_weight, "seq", axis=0, tiled=True),
    )
    x_total = jnp.dot(hidden, x_rows, preferred_element_type=jnp.float32)
    bc_total = jnp.dot(hidden, bc_rows, preferred_element_type=jnp.float32)
    dt_total = jnp.dot(hidden, dt_rows, preferred_element_type=jnp.float32)
    inputs = x_total.astype(jnp.bfloat16).reshape(tok_rows, heads, P_SIZE)
    maps = lax.all_gather(bc_total.astype(jnp.bfloat16), "rep", axis=1, tiled=True)
    b_all = maps[:, :NS]
    c_all = maps[:, NS:]
    steps = jax.nn.softplus(dt_total + dt_bias)
    rates = -steps * decay_rate
    state = jnp.zeros((heads, NS, P_SIZE), jnp.float32)
    prev_seg = jnp.int32(-1)
    result, state, prev_seg = block_step(
        state, prev_seg, inputs, b_all, c_all, steps, rates, seg_ids
    )
    whole_keep = jnp.exp(jnp.sum(rates, axis=0)) * (seg_ids[0] == seg_ids[tok_rows - 1]).astype(
        jnp.float32
    )
    element = (state, whole_keep, seg_ids[:1], seg_ids[tok_rows - 1 :])
    reach = DOC_MAX // tok_rows + 1
    first_hop = passed_along((element[0], element[1], element[2], element[3]), "seq", 1)
    incoming = first_hop
    for hop in range(reach - 1):
        incoming = combine(
            passed_along((incoming[0], incoming[1], incoming[2], incoming[3]), "seq", 1), first_hop
        )
    state_in = incoming[0]
    tag_in = incoming[3]
    running = jnp.cumsum(rates, axis=0)
    factor = jnp.exp(running) * (seg_ids == tag_in[0]).astype(jnp.float32)[:, None]
    extra = state_read(c_all, state_in) * factor[:, :, None]
    total_out = result + extra + skip[None, :, None] * inputs.astype(jnp.float32)
    return total_out.astype(jnp.bfloat16).reshape(tok_rows, width)


def pick(first, one, other):
    return jnp.where(first, one, other)


def call(body, outs, *operands, flops=0, scratch=()):
    single = not isinstance(outs, list)
    shapes = [outs] if single else outs
    size = sum(math.prod(o.shape) * o.dtype.itemsize for o in (*operands, *shapes))
    result = pl.pallas_call(
        body,
        out_shape=shapes,
        in_specs=[pl.BlockSpec(memory_space=pltpu.SMEM)]
        + [pl.BlockSpec(memory_space=pltpu.VMEM)] * (len(operands) - 1),
        out_specs=[pl.BlockSpec(memory_space=pltpu.VMEM)] * len(shapes),
        scratch_shapes=list(scratch),
        compiler_params=pltpu.CompilerParams(vmem_limit_bytes=40 * 2**20),
        cost_estimate=pl.CostEstimate(flops=flops, bytes_accessed=size, transcendentals=0),
    )(*operands)
    return result[0] if single else result


def contract_last(a, b):
    return lax.dot_general(a, b, (((1,), (1,)), ((), ())), preferred_element_type=jnp.float32)


def mul(a, b):
    return jnp.dot(a, b, preferred_element_type=jnp.float32)


def depth_blocks(place, token_refs, at, size):
    hidden_ref, near_ref, far_ref = token_refs
    own = hidden_ref[:, pl.ds(pl.multiple_of(at * size, size), size)]
    blocks = near_ref.shape[1] // size
    inside = pl.ds(pl.multiple_of((at % blocks) * size, size), size)
    is_near = (at // blocks) == place[2]
    return own, jnp.where(is_near, near_ref[:, inside], far_ref[:, inside])


def share_kernel(used, place, hidden, near, far, s0, s1, s2, s3, out):
    plane, lane = place[0], place[1]
    rows = hidden.shape[0]
    size = s0.shape[1]
    totals = [None, None]
    for back, s in enumerate((s0, s1, s2, s3)):
        at = LANES * ((plane + PLANES - back) % PLANES) + lane
        weights = s[...]
        for r, tokens in enumerate(depth_blocks(place, (hidden, near, far), at, size)):
            product = contract_last(weights, tokens)
            totals[r] = product if totals[r] is None else totals[r] + product
    row = lax.broadcasted_iota(jnp.int32, (s0.shape[0] - used, rows), 0)
    ids = s0[used:, :rows].astype(jnp.float32)
    ends = [s[used:, :rows].astype(jnp.float32)[0:1, rows - 1 : rows] for s in (s1, s2)]
    notes = jnp.where(row == 1, ends[0], jnp.where(row == 2, ends[1], ids))
    out[:used, :rows] = totals[0][:used]
    out[:used, rows:] = totals[1][:used]
    out[used:, :rows] = notes
    out[used:, rows:] = jnp.zeros_like(notes)


def decay_kernel(
    map_cols, place, maps, total, bias, rate_of, mixing, loaded, c_out, fac, meta
):
    f32, bf16 = jnp.float32, jnp.bfloat16
    plane, lane = place[0], place[1]
    heads = bias.shape[0]
    mine = heads // 2
    rows = total.shape[1] // 2
    even = lane == 0
    pre = total[map_cols : map_cols + heads, :] + bias[...]
    steps = jnp.maximum(pre, 0.0) + jnp.log1p(jnp.exp(-jnp.abs(pre)))
    rates = -steps * rate_of[...]
    steps = jnp.where(even, steps[:mine], steps[mine:])
    rates = jnp.where(even, rates[:mine], rates[mine:])
    notes = total[map_cols + heads :, :]
    tri_row = lax.broadcasted_iota(jnp.int32, (rows, rows), 0)
    tri_col = lax.broadcasted_iota(jnp.int32, (rows, rows), 1)
    upper = (tri_row <= tri_col).astype(f32)
    causal = tri_row >= tri_col
    pad = jnp.zeros((8 - mine, rows), f32)
    cums, lasts = [], []
    for r in range(2):
        cut = slice(r * rows, (r + 1) * rows)
        cums.append(
            lax.dot_general(
                jnp.concatenate([rates[:, cut], pad], axis=0),
                upper,
                (((1,), (0,)), ((), ())),
                precision=lax.Precision.HIGHEST,
                preferred_element_type=f32,
            )
        )
        lasts.append(notes[0:1, (r + 1) * rows - 1 : (r + 1) * rows])
    end = [c[:mine, rows - 1 : rows] for c in cums]
    end0, end1 = pick(even, end[0], end[1]), pick(even, end[1], end[0])
    last0, last1 = pick(even, lasts[0], lasts[1]), pick(even, lasts[1], lasts[0])
    final = pick(even, notes[:, 2 * rows - 1 :], notes[:, rows - 1 : rows])
    tag = jnp.where(plane > 0, final[1:2], -1.0)
    tag_before = jnp.where(plane > 1, final[2:3], -1.0)
    link = jnp.exp(end1) * (last1 == last0).astype(f32)
    enters = jnp.exp(end0) * (last0 == tag).astype(f32)
    through = jnp.exp(end0 + end1)
    passes = (tag == tag_before).astype(f32)
    width = meta.shape[1] // mine
    meta[...] = jnp.zeros_like(meta)
    for h in range(mine):
        cut = slice(h * width, (h + 1) * width)
        meta[0:1, cut] = jnp.broadcast_to(link[h : h + 1], (1, width))
        meta[1:2, cut] = jnp.broadcast_to(enters[h : h + 1], (1, width))
        meta[2:3, cut] = jnp.broadcast_to(through[h : h + 1], (1, width))
        meta[3:4, cut] = jnp.broadcast_to(passes, (1, width))
    for r in range(2):
        b = lane if r == 0 else 1 - lane
        cut = slice(r * rows, (r + 1) * rows)
        seg, cum, dt = notes[0:1, cut], cums[r], steps[:, cut]
        source = jnp.where(b == 0, tag, last0)
        factor = jnp.exp(cum) * (seg == source).astype(f32)
        fac[b] = factor.T
        cols = jnp.concatenate([cum[:mine], jnp.broadcast_to(seg, (8 - mine, rows))], axis=0).T
        keep = causal & (cols[:, mine : mine + 1] == seg)
        b_t, c_t = maps[:NS, cut], maps[NS:, cut]
        c_rows = c_t.astype(f32).T.astype(bf16)
        c_out[b] = c_rows
        scores = mul(c_rows, b_t)
        tail = jnp.exp(end[r] - cum[:mine]) * dt * (seg == lasts[r]).astype(f32)
        wide = b_t.astype(f32)
        for h in range(mine):
            gap = cols[:, h : h + 1] - cum[h : h + 1]
            decay = jnp.where(keep, jnp.exp(jnp.where(keep, gap, 0.0)), 0.0)
            mixing[b, h] = (scores * decay * dt[h : h + 1]).astype(bf16)
            loaded[b, h] = (wide * tail[h : h + 1]).astype(bf16)


def add_products(place, token_refs, backs, weight_refs, totals):
    plane, lane = place[0], place[1]
    for (back, is_own), w in zip(backs, weight_refs):
        at = LANES * ((plane + PLANES - back) % PLANES) + (lane if is_own else 1 - lane)
        weights = w[...]
        for r, tokens in enumerate(depth_blocks(place, token_refs, at, w.shape[0])):
            product = mul(tokens, weights)
            totals[r] = product if totals[r] is None else totals[r] + product


def early_kernel(backs, place, hidden, near, far, *refs):
    *weights, out = refs
    totals = [None, None]
    if len(weights) > len(backs):
        totals = [weights[0][0], weights[0][1]]
        weights = weights[1:]
    add_products(place, (hidden, near, far), backs, weights, totals)
    out[0] = totals[0]
    out[1] = totals[1]


def input_kernel(place, hidden, near, far, acc, last_own, last_other, loaded, meta, x_out, ready, built_out):
    f32, bf16 = jnp.float32, jnp.bfloat16
    lane = place[1]
    totals = [acc[0], acc[1]]
    backs = ((PLANES - 1, True), (PLANES - 1, False))
    add_products(place, (hidden, near, far), backs, (last_own, last_other), totals)
    x_out[lane] = totals[0].astype(bf16)
    x_out[1 - lane] = totals[1].astype(bf16)
    mine = loaded.shape[1]
    width = meta.shape[1] // mine
    for h in range(mine):
        cut = slice(h * width, (h + 1) * width)
        first = mul(loaded[0, h], x_out[0, :, cut])
        second = mul(loaded[1, h], x_out[1, :, cut])
        ready[:NS, cut] = (second + meta[0:1, cut] * first).astype(bf16)
        built_out[:, cut] = first.astype(bf16)
    through = meta[2:3, :]
    upper = through.astype(bf16)
    lower = (through - upper.astype(f32)).astype(bf16)
    row = lax.broadcasted_iota(jnp.int32, (ready.shape[0] - NS, ready.shape[1]), 0)
    ready[NS:, :] = jnp.where(
        row == 0, upper.astype(f32), jnp.where(row == 1, lower.astype(f32), 0.0)
    ).astype(bf16)


def local_kernel(place, x, mixing, skip, c_rows, built, fac, out):
    lane = place[1]
    mine = mixing.shape[1]
    width = x.shape[2] // mine
    carried = mul(c_rows[1], built[...])
    gains = jnp.where(lane == 0, skip[:, :mine], skip[:, mine:])
    for h in range(mine):
        cut = slice(h * width, (h + 1) * width)
        for b in range(2):
            xs = x[b, :, cut]
            local = mul(mixing[b, h], xs) + gains[:, h : h + 1] * xs.astype(jnp.float32)
            if b == 1:
                local = local + fac[1, :, h : h + 1] * carried[:, cut]
            out[b, :, cut] = local


def final_kernel(partner, mine, place, local, c_rows, fac, meta, one, two, out):
    f32, bf16 = jnp.float32, jnp.bfloat16
    lane = place[1]
    b = 1 - lane if partner else lane
    through = one[NS : NS + 1, :].astype(f32) + one[NS + 1 : NS + 2, :].astype(f32)
    incoming = one[:NS, :].astype(f32) + (through * meta[3:4, :]) * two[:NS, :].astype(f32)
    entering = (incoming * jnp.where(b == 1, meta[1:2, :], 1.0)).astype(bf16)
    carried = mul(c_rows[b], entering)
    factor = fac[b]
    width = out.shape[1] // mine
    for h in range(mine):
        cut = slice(h * width, (h + 1) * width)
        out[:, cut] = (local[b, :, cut] + factor[:, h : h + 1] * carried[:, cut]).astype(bf16)


def plane_shards(hidden, seg_ids, x_weight, bc_weight, dt_weight, dt_bias, decay_rate, skip):
    bf16, f32 = jnp.bfloat16, jnp.float32
    me = lax.axis_index("seq")
    lane, plane = me % LANES, me // LANES
    even = lane == 0
    core = lax.axis_index("rep") % 2
    place = jnp.stack([plane, lane, core]).astype(jnp.int32)
    rows, depth = hidden.shape
    k_rows, cols = x_weight.shape
    half = cols // 2
    heads = dt_bias.shape[0]
    mine = heads // 2
    map_cols = bc_weight.shape[1]
    used = map_cols + heads

    def shaped(dtype, *shape):
        return jax.ShapeDtypeStruct(shape, dtype)

    def at(p, l):
        return LANES * p + l

    swap = [(i, i ^ 1) for i in range(LANES * PLANES)]
    cores = [(i, i ^ 1) for i in range(lax.axis_size("rep"))]

    def shift(by, sources):
        return [(at(p, l), at(p + by, l)) for p in sources for l in range(LANES)]

    def ring(by):
        return [(at(p, l), at((p + by) % PLANES, l)) for p in range(PLANES) for l in range(LANES)]

    def send(x, pairs, axis="seq"):
        return lax.ppermute(x, axis, pairs)

    together = lax.optimization_barrier
    along = ring(1)

    def add_early(backs, *operands):
        return call(
            functools.partial(early_kernel, backs),
            shaped(f32, LANES, rows, half),
            place,
            hidden,
            near,
            far,
            *operands,
            flops=4 * rows * k_rows * half * len(backs),
        )

    own = pick(even, x_weight[:, :half], x_weight[:, half:])
    other = send(pick(even, x_weight[:, half:], x_weight[:, :half]), swap)
    own_one = send(own, along)
    other_one = send(other, along)
    own_two = send(own_one, along)
    other_two = send(other_one, along)
    own_three = send(own_two, along)
    other_three = send(other_two, along)

    ids_row = jnp.pad(seg_ids.astype(bf16), (0, k_rows - rows))[None]
    small = jnp.concatenate(
        [bc_weight.T, dt_weight.T, ids_row, jnp.zeros((7, k_rows), bf16)], axis=0
    )
    near = pick(core == 0, hidden[:, : depth // 2], hidden[:, depth // 2 :])
    from_ring = [send(small, ring(by)) for by in (1, 2, 3)]
    near, from_ring, _ = together((near, from_ring, (other, own_one)))
    near = send(near, swap)
    near, from_ring, _ = together((near, from_ring, (own_two, other_one)))
    far = send(near, cores, "rep")
    share = call(
        functools.partial(share_kernel, used),
        shaped(f32, used + 8, LANES * rows),
        place,
        hidden,
        near,
        far,
        small,
        *from_ring,
        flops=4 * rows * depth * used,
    )
    early = add_early(
        ((0, True), (0, False), (1, True), (1, False)), own, other, own_one, other_one
    )
    share_other = send(share, swap)
    total = share + jnp.concatenate([share_other[:, rows:], share_other[:, :rows]], axis=1)
    total, _ = together((total, own_three))
    maps = lax.all_gather(total[:map_cols].astype(bf16), "rep", axis=0, tiled=True)
    mixing, loaded, c_rows, fac, meta = call(
        functools.partial(decay_kernel, map_cols),
        [
            shaped(bf16, LANES, mine, rows, rows),
            shaped(bf16, LANES, mine, NS, rows),
            shaped(bf16, LANES, rows, NS),
            shaped(f32, LANES, rows, 8),
            shaped(f32, 8, half),
        ],
        place,
        maps,
        total,
        dt_bias[:, None],
        decay_rate[:, None],
        flops=100 * mine * rows * rows,
    )
    early = add_early(((2, True), (2, False)), early, own_two, other_two)
    inputs, ready, built = call(
        input_kernel,
        [
            shaped(bf16, LANES, rows, half),
            shaped(bf16, NS + 16, half),
            shaped(bf16, NS, half),
        ],
        place,
        hidden,
        near,
        far,
        early,
        own_three,
        other_three,
        loaded,
        meta,
        flops=rows * depth * half,
    )
    from_one = send(ready, shift(1, (0, 1, 2)))
    from_two = send(ready, shift(2, (0, 1)))
    local = call(
        local_kernel,
        shaped(f32, LANES, rows, half),
        place,
        inputs,
        mixing,
        skip[None],
        c_rows,
        built,
        fac,
        flops=4 * rows * rows * half,
    )

    def finish(partner):
        return call(
            functools.partial(final_kernel, partner, mine),
            shaped(bf16, rows, half),
            place,
            local,
            c_rows,
            fac,
            meta,
            from_one,
            from_two,
            flops=2 * rows * NS * half,
        )

    swapped = send(finish(True), swap)
    kept = finish(False)
    return pick(
        even,
        jnp.concatenate([kept, swapped], axis=1),
        jnp.concatenate([swapped, kept], axis=1),
    )


def solution(mesh):
    placed = (
        P("seq", None),
        P("seq"),
        P("seq", "rep"),
        P("seq", "rep"),
        P("seq", "rep"),
        P("rep"),
        P("rep"),
        P("rep"),
    )
    by_planes = mesh.shape["seq"] == LANES * PLANES and mesh.shape["rep"] % 2 == 0
    return jax.shard_map(
        plane_shards if by_planes else gathered_shards,
        mesh=mesh,
        in_specs=placed,
        out_specs=P("seq", "rep"),
        check_vma=False,
    )
```

```python
import functools
import math

import jax
import jax.numpy as jnp
from jax import lax
from jax.experimental import pallas as pl
from jax.experimental.pallas import tpu as pltpu
from jax.sharding import PartitionSpec as P

P_SIZE = 128
NS = 128
DOC_MAX = 1024
LANES = 2
PLANES = 4
SUBLANES = 8


def passed_along(x, axis, by):
    peers = lax.axis_size(axis)
    pairs = [(i, i + by) for i in range(peers) if 0 <= i + by < peers]
    return lax.ppermute(x, axis, pairs)


def state_read(c_block, state):
    upper_part = state.astype(jnp.bfloat16)
    lower_part = (state - upper_part.astype(jnp.float32)).astype(jnp.bfloat16)
    first = jnp.einsum("tn,hnp->thp", c_block, upper_part, preferred_element_type=jnp.float32)
    second = jnp.einsum("tn,hnp->thp", c_block, lower_part, preferred_element_type=jnp.float32)
    return first + second


def block_step(state, prev_seg, x_block, b_block, c_block, dt_block, rate_block, seg_block):
    count = x_block.shape[0]
    cum = jnp.cumsum(rate_block, axis=0)
    order = jnp.arange(count)
    masked = (order[:, None] >= order[None, :]) & (seg_block[:, None] == seg_block[None, :])
    scores = jnp.dot(c_block, b_block.T, preferred_element_type=jnp.float32)
    cum_heads = cum.T
    gaps = cum_heads[:, :, None] - cum_heads[:, None, :]
    decay = jnp.where(masked[None], jnp.exp(jnp.where(masked[None], gaps, 0.0)), 0.0)
    mixing = (scores[None] * decay * dt_block.T[:, None, :]).astype(jnp.bfloat16)
    diag_part = jnp.einsum("htj,jhp->thp", mixing, x_block, preferred_element_type=jnp.float32)
    keep = (seg_block == prev_seg).astype(jnp.float32)
    factor = jnp.exp(cum) * keep[:, None]
    carried = state_read(c_block, state) * factor[:, :, None]
    last_seg = seg_block[count - 1]
    tail = (
        jnp.exp(cum[count - 1][None, :] - cum)
        * dt_block
        * (seg_block == last_seg).astype(jnp.float32)[:, None]
    )
    loaded = (tail.T[:, :, None] * b_block.astype(jnp.float32)[None]).astype(jnp.bfloat16)
    built = jnp.einsum("hjn,jhp->hnp", loaded, x_block, preferred_element_type=jnp.float32)
    through = jnp.exp(cum[count - 1]) * (last_seg == prev_seg).astype(jnp.float32)
    new_state = built + through[:, None, None] * state
    return (diag_part + carried, new_state, last_seg)


def combine(earlier, later):
    early_state, early_keep, early_first, early_last = earlier
    late_state, late_keep, late_first, late_last = later
    linked = ((early_last == late_first) | (early_last < 0) | (late_first < 0)).astype(jnp.float32)
    passing = late_keep * linked
    return (
        late_state + passing[:, None, None] * early_state,
        early_keep * passing,
        jnp.where(early_first < 0, late_first, early_first),
        jnp.where(late_last < 0, early_last, late_last),
    )


def gathered_shards(hidden, seg_ids, x_weight, bc_weight, dt_weight, dt_bias, decay_rate, skip):
    tok_rows = hidden.shape[0]
    heads = dt_bias.shape[0]
    width = x_weight.shape[1]
    x_rows, bc_rows, dt_rows = (
        lax.all_gather(x_weight, "seq", axis=0, tiled=True),
        lax.all_gather(bc_weight, "seq", axis=0, tiled=True),
        lax.all_gather(dt_weight, "seq", axis=0, tiled=True),
    )
    x_total = jnp.dot(hidden, x_rows, preferred_element_type=jnp.float32)
    bc_total = jnp.dot(hidden, bc_rows, preferred_element_type=jnp.float32)
    dt_total = jnp.dot(hidden, dt_rows, preferred_element_type=jnp.float32)
    inputs = x_total.astype(jnp.bfloat16).reshape(tok_rows, heads, P_SIZE)
    maps = lax.all_gather(bc_total.astype(jnp.bfloat16), "rep", axis=1, tiled=True)
    b_all = maps[:, :NS]
    c_all = maps[:, NS:]
    steps = jax.nn.softplus(dt_total + dt_bias)
    rates = -steps * decay_rate
    state = jnp.zeros((heads, NS, P_SIZE), jnp.float32)
    prev_seg = jnp.int32(-1)
    result, state, prev_seg = block_step(
        state, prev_seg, inputs, b_all, c_all, steps, rates, seg_ids
    )
    whole_keep = jnp.exp(jnp.sum(rates, axis=0)) * (seg_ids[0] == seg_ids[tok_rows - 1]).astype(
        jnp.float32
    )
    element = (state, whole_keep, seg_ids[:1], seg_ids[tok_rows - 1 :])
    reach = DOC_MAX // tok_rows + 1
    first_hop = passed_along((element[0], element[1], element[2], element[3]), "seq", 1)
    incoming = first_hop
    for hop in range(reach - 1):
        incoming = combine(
            passed_along((incoming[0], incoming[1], incoming[2], incoming[3]), "seq", 1), first_hop
        )
    state_in = incoming[0]
    tag_in = incoming[3]
    running = jnp.cumsum(rates, axis=0)
    factor = jnp.exp(running) * (seg_ids == tag_in[0]).astype(jnp.float32)[:, None]
    extra = state_read(c_all, state_in) * factor[:, :, None]
    total_out = result + extra + skip[None, :, None] * inputs.astype(jnp.float32)
    return total_out.astype(jnp.bfloat16).reshape(tok_rows, width)


def pick(first, one, other):
    return jnp.where(first, one, other)


def call(body, outs, *operands, flops=0, scratch=(), left=0, grant=16):
    single = not isinstance(outs, list)
    shapes = [outs] if single else outs
    size = sum(math.prod(o.shape) * o.dtype.itemsize for o in (*operands, *shapes))
    result = pl.pallas_call(
        body,
        out_shape=shapes,
        in_specs=[pl.BlockSpec(memory_space=pltpu.SMEM)]
        + [pl.BlockSpec(memory_space=pltpu.VMEM)] * (len(operands) - 1 - left)
        + [pl.BlockSpec(memory_space=pl.ANY)] * left,
        out_specs=[pl.BlockSpec(memory_space=pltpu.VMEM)] * len(shapes),
        scratch_shapes=list(scratch),
        compiler_params=pltpu.CompilerParams(vmem_limit_bytes=grant * 2**20),
        cost_estimate=pl.CostEstimate(flops=flops, bytes_accessed=size, transcendentals=0),
    )(*operands)
    return result[0] if single else result


def contract_last(a, b):
    return lax.dot_general(a, b, (((1,), (1,)), ((), ())), preferred_element_type=jnp.float32)


def mul(a, b):
    return jnp.dot(a, b, preferred_element_type=jnp.float32)


def depth_blocks(place, token_refs, at, size):
    hidden_ref, near_ref, far_ref = token_refs
    own = hidden_ref[:, pl.ds(pl.multiple_of(at * size, size), size)]
    blocks = near_ref.shape[1] // size
    inside = pl.ds(pl.multiple_of((at % blocks) * size, size), size)
    is_near = (at // blocks) == place[2]
    return own, jnp.where(is_near, near_ref[:, inside], far_ref[:, inside])


def split_kernel(place, x_weight, bc, dt, ids, hidden, own, sent, small, ahead, below, ids_in, done):
    f32, bf16 = jnp.float32, jnp.bfloat16
    plane, lane, core = place[0], place[1], place[2]
    size, half = x_weight.shape[0], x_weight.shape[1] // 2
    maps, heads, rows = bc.shape[0], dt.shape[0], ids.shape[1]
    at = LANES * ((plane + 1) % PLANES) + core

    def columns(ref, index, width):
        return ref.at[:, pl.ds(pl.multiple_of(index * width, width), width)]

    moves = [
        (columns(hidden, at, size), ahead),
        (columns(x_weight, lane, half), own.at[pl.ds(0, size), :]),
        (columns(x_weight, 1 - lane, half), sent),
        (bc, own.at[pl.ds(size, maps), :]),
        (bc, small.at[pl.ds(0, maps), :]),
        (dt, below),
        (ids, ids_in),
    ]
    copies = [pltpu.make_async_copy(a, b, done.at[i]) for i, (a, b) in enumerate(moves)]
    for copy in copies:
        copy.start()
    for copy in copies:
        copy.wait()
    row = lax.broadcasted_iota(jnp.int32, (heads, rows), 0)
    notes = jnp.where(row == 0, ids_in[...].astype(f32), 0.0)
    notes = jnp.concatenate([notes, jnp.zeros((heads, size - rows), f32)], axis=1)
    last = jnp.concatenate([below[...].astype(f32), notes], axis=0).astype(bf16)
    own[size + maps :, :] = last
    small[maps:, :] = last


def share_kernel(used, place, hidden, near, far, c0, c1, c2, s3, out, small, done):
    plane, lane = place[0], place[1]
    rows = hidden.shape[0]
    size = c0.shape[1]
    below = pl.ds(size, c0.shape[0] - size)
    copies = [
        pltpu.make_async_copy(c.at[below, :], small.at[i], done.at[i])
        for i, c in enumerate((c0, c1, c2))
    ]
    copies.append(pltpu.make_async_copy(s3, small.at[3], done.at[3]))
    for copy in copies:
        copy.start()
    totals = [None, None]
    for back, copy in enumerate(copies):
        at = LANES * ((plane + PLANES - back) % PLANES) + lane
        copy.wait()
        weights = small[back]
        for r, tokens in enumerate(depth_blocks(place, (hidden, near, far), at, size)):
            product = contract_last(weights, tokens)
            totals[r] = product if totals[r] is None else totals[r] + product
    notes = [small[i, used:, :rows].astype(jnp.float32) for i in range(3)]
    row = lax.broadcasted_iota(jnp.int32, notes[0].shape, 0)
    ends = [n[0:1, rows - 1 : rows] for n in notes[1:]]
    note = jnp.where(row == 1, ends[0], jnp.where(row == 2, ends[1], notes[0]))
    out[:used, :rows] = totals[0][:used]
    out[:used, rows:] = totals[1][:used]
    out[used:, :rows] = note
    out[used:, rows:] = jnp.zeros_like(note)


def decay_kernel(
    map_cols, place, some, some_core, some_chip, some_both, total, bias, rate_of, mixing, loaded, c_out, fac, meta
):
    f32, bf16 = jnp.float32, jnp.bfloat16
    plane, lane = place[0], place[1]
    first_core, first_chip = place[2] == 0, place[3] == 0
    here = [pick(first_core, a[...], b[...]) for a, b in ((some, some_core), (some_core, some))]
    there = [
        pick(first_core, a[...], b[...])
        for a, b in ((some_chip, some_both), (some_both, some_chip))
    ]
    here, there = jnp.concatenate(here, axis=0), jnp.concatenate(there, axis=0)
    b_maps, c_maps = pick(first_chip, here, there), pick(first_chip, there, here)
    heads = bias.shape[0]
    mine = heads // 2
    rows = total.shape[1] // 2
    even = lane == 0
    pre = total[map_cols : map_cols + heads, :] + bias[...]
    steps = jnp.maximum(pre, 0.0) + jnp.log1p(jnp.exp(-jnp.abs(pre)))
    rates = -steps * rate_of[...]
    steps = jnp.where(even, steps[:mine], steps[mine:])
    rates = jnp.where(even, rates[:mine], rates[mine:])
    notes = total[map_cols + heads :, :]
    tri_row = lax.broadcasted_iota(jnp.int32, (rows, rows), 0)
    tri_col = lax.broadcasted_iota(jnp.int32, (rows, rows), 1)
    upper = (tri_row <= tri_col).astype(f32)
    causal = tri_row >= tri_col
    pad = jnp.zeros((8 - mine, rows), f32)
    cums, lasts = [], []
    for r in range(2):
        cut = slice(r * rows, (r + 1) * rows)
        cums.append(
            lax.dot_general(
                jnp.concatenate([rates[:, cut], pad], axis=0),
                upper,
                (((1,), (0,)), ((), ())),
                precision=lax.Precision.HIGHEST,
                preferred_element_type=f32,
            )
        )
        lasts.append(notes[0:1, (r + 1) * rows - 1 : (r + 1) * rows])
    end = [c[:mine, rows - 1 : rows] for c in cums]
    end0, end1 = pick(even, end[0], end[1]), pick(even, end[1], end[0])
    last0, last1 = pick(even, lasts[0], lasts[1]), pick(even, lasts[1], lasts[0])
    final = pick(even, notes[:, 2 * rows - 1 :], notes[:, rows - 1 : rows])
    tag = jnp.where(plane > 0, final[1:2], -1.0)
    tag_before = jnp.where(plane > 1, final[2:3], -1.0)
    link = jnp.exp(end1) * (last1 == last0).astype(f32)
    enters = jnp.exp(end0) * (last0 == tag).astype(f32)
    through = jnp.exp(end0 + end1)
    passes = (tag == tag_before).astype(f32)
    width = meta.shape[1] // mine
    meta[...] = jnp.zeros_like(meta)
    for h in range(mine):
        cut = slice(h * width, (h + 1) * width)
        meta[0:1, cut] = jnp.broadcast_to(link[h : h + 1], (1, width))
        meta[1:2, cut] = jnp.broadcast_to(enters[h : h + 1], (1, width))
        meta[2:3, cut] = jnp.broadcast_to(through[h : h + 1], (1, width))
        meta[3:4, cut] = jnp.broadcast_to(passes, (1, width))
    for r in range(2):
        b = lane if r == 0 else 1 - lane
        cut = slice(r * rows, (r + 1) * rows)
        seg, cum, dt = notes[0:1, cut], cums[r], steps[:, cut]
        source = jnp.where(b == 0, tag, last0)
        factor = jnp.exp(cum) * (seg == source).astype(f32)
        fac[b] = factor.T
        cols = jnp.concatenate([cum[:mine], jnp.broadcast_to(seg, (8 - mine, rows))], axis=0).T
        keep = causal & (cols[:, mine : mine + 1] == seg)
        b_t, c_t = b_maps[:, cut], c_maps[:, cut]
        c_rows = c_t.astype(f32).T.astype(bf16)
        c_out[b] = c_rows
        scores = mul(c_rows, b_t)
        tail = jnp.exp(end[r] - cum[:mine]) * dt * (seg == lasts[r]).astype(f32)
        wide = b_t.astype(f32)
        for h in range(mine):
            gap = cols[:, h : h + 1] - cum[h : h + 1]
            decay = jnp.where(keep, jnp.exp(jnp.where(keep, gap, 0.0)), 0.0)
            mixing[b, h] = (scores * decay * dt[h : h + 1]).astype(bf16)
            loaded[b, h] = (wide * tail[h : h + 1]).astype(bf16)


def add_products(place, token_refs, backs, weight_refs, totals):
    plane, lane = place[0], place[1]
    for (back, is_own), w in zip(backs, weight_refs):
        at = LANES * ((plane + PLANES - back) % PLANES) + (lane if is_own else 1 - lane)
        size = w.shape[1]
        weights = w[:size, :]
        for r, tokens in enumerate(depth_blocks(place, token_refs, at, size)):
            product = mul(tokens, weights)
            totals[r] = product if totals[r] is None else totals[r] + product


def early_kernel(backs, place, hidden, near, far, *refs):
    *weights, out = refs
    totals = [None, None]
    if len(weights) > len(backs):
        totals = [weights[0][0], weights[0][1]]
        weights = weights[1:]
    add_products(place, (hidden, near, far), backs, weights, totals)
    out[0] = totals[0]
    out[1] = totals[1]


def neighbour_kernel(place, mine, far, own, other, out):
    same = place[1] == place[2]
    size = other.shape[0]
    here, there = mine[...], far[...]
    first, second = jnp.where(same, here, there), jnp.where(same, there, here)
    out[...] = (mul(first, own[:size, :]) + mul(second, other[...])).astype(out.dtype)


def input_kernel(backs, place, hidden, near, far, acc, back, *refs):
    *chunks, loaded, meta, x_out, ready, built_out = refs
    f32, bf16 = jnp.float32, jnp.bfloat16
    lane = place[1]
    rows = hidden.shape[0]
    totals = [acc[0] + back[:rows, :].astype(f32), acc[1] + back[rows : 2 * rows, :].astype(f32)]
    add_products(place, (hidden, near, far), backs, chunks, totals)
    x_out[lane] = totals[0].astype(bf16)
    x_out[1 - lane] = totals[1].astype(bf16)
    mine = loaded.shape[1]
    width = meta.shape[1] // mine
    for h in range(mine):
        cut = slice(h * width, (h + 1) * width)
        first = mul(loaded[0, h], x_out[0, :, cut])
        second = mul(loaded[1, h], x_out[1, :, cut])
        ready[:NS, cut] = (second + meta[0:1, cut] * first).astype(bf16)
        built_out[:, cut] = first.astype(bf16)
    through = meta[2:3, :]
    upper = through.astype(bf16)
    lower = (through - upper.astype(f32)).astype(bf16)
    row = lax.broadcasted_iota(jnp.int32, (ready.shape[0] - NS, ready.shape[1]), 0)
    ready[NS:, :] = jnp.where(
        row == 0, upper.astype(f32), jnp.where(row == 1, lower.astype(f32), 0.0)
    ).astype(bf16)


def local_kernel(place, x, mixing, skip, c_rows, built, fac, out):
    lane = place[1]
    mine = mixing.shape[1]
    width = x.shape[2] // mine
    carried = mul(c_rows[1], built[...])
    gains = jnp.where(lane == 0, skip[:, :mine], skip[:, mine:])
    for h in range(mine):
        cut = slice(h * width, (h + 1) * width)
        for b in range(2):
            xs = x[b, :, cut]
            local = mul(mixing[b, h], xs) + gains[:, h : h + 1] * xs.astype(jnp.float32)
            if b == 1:
                local = local + fac[1, :, h : h + 1] * carried[:, cut]
            out[b, :, cut] = local


def final_kernel(partner, mine, place, local, c_rows, fac, meta, one, two, out):
    f32, bf16 = jnp.float32, jnp.bfloat16
    lane = place[1]
    b = 1 - lane if partner else lane
    through = one[NS : NS + 1, :].astype(f32) + one[NS + 1 : NS + 2, :].astype(f32)
    incoming = one[:NS, :].astype(f32) + (through * meta[3:4, :]) * two[:NS, :].astype(f32)
    entering = (incoming * jnp.where(b == 1, meta[1:2, :], 1.0)).astype(bf16)
    carried = mul(c_rows[b], entering)
    factor = fac[b]
    width = out.shape[1] // mine
    for h in range(mine):
        cut = slice(h * width, (h + 1) * width)
        out[:, cut] = (local[b, :, cut] + factor[:, h : h + 1] * carried[:, cut]).astype(bf16)


def plane_shards(hidden, seg_ids, x_weight, bc_weight, dt_weight, dt_bias, decay_rate, skip):
    bf16, f32 = jnp.bfloat16, jnp.float32
    me = lax.axis_index("seq")
    lane, plane = me % LANES, me // LANES
    even = lane == 0
    core = lax.axis_index("rep") % 2
    place = jnp.stack([plane, lane, core, lax.axis_index("rep") // 2]).astype(jnp.int32)
    rows, depth = hidden.shape
    k_rows, cols = x_weight.shape
    half = cols // 2
    heads = dt_bias.shape[0]
    mine = heads // 2
    map_cols = bc_weight.shape[1]
    used = map_cols + heads

    def shaped(dtype, *shape):
        return jax.ShapeDtypeStruct(shape, dtype)

    def at(p, l):
        return LANES * p + l

    swap = [(i, i ^ 1) for i in range(LANES * PLANES)]
    cores = [(i, i ^ 1) for i in range(lax.axis_size("rep"))]
    chips = [(i, i ^ 2) for i in range(lax.axis_size("rep"))]

    def shift(by, sources):
        return [(at(p, l), at(p + by, l)) for p in sources for l in range(LANES)]

    along = [(at(p, l), at((p + 1) % PLANES, l)) for p in range(PLANES) for l in range(LANES)]
    back = [(b, a) for a, b in along]

    def send(x, pairs, axis="seq"):
        return lax.ppermute(x, axis, pairs)

    together = lax.optimization_barrier

    own, sent, small, ahead = call(
        split_kernel,
        [
            shaped(bf16, k_rows + used + heads, half),
            shaped(bf16, k_rows, half),
            shaped(bf16, used + heads, k_rows),
            shaped(bf16, rows, k_rows),
        ],
        place,
        x_weight,
        bc_weight.T,
        dt_weight.T,
        seg_ids[None],
        hidden,
        left=5,
        grant=60,
        scratch=[
            pltpu.VMEM((heads, k_rows), bf16),
            pltpu.VMEM((1, rows), jnp.int32),
            pltpu.SemaphoreType.DMA((7,)),
        ],
    )
    ahead = send(ahead, along)
    other = send(sent, swap)
    own_one = send(own, along)
    small_next = send(small, back)
    near = pick(core == 0, hidden[:, : depth // 2], hidden[:, depth // 2 :])
    ahead_other = send(ahead, swap)
    other, own_one, near, ahead, ahead_other = together((other, own_one, near, ahead, ahead_other))

    other_one = send(other, along)
    own_two = send(own_one, along)
    near = send(near, swap)
    ahead = jnp.concatenate([ahead, ahead_other], axis=0)
    ahead_far = send(ahead, cores, "rep")
    part = call(
        neighbour_kernel,
        shaped(bf16, LANES * rows, half),
        place,
        ahead,
        ahead_far,
        own,
        other,
        flops=4 * rows * LANES * k_rows * half,
    )
    other_one, own_two, near, part = together((other_one, own_two, near, part))

    other_two = send(other_one, along)
    from_next = send(part, back)
    far = send(near, cores, "rep")
    share = call(
        functools.partial(share_kernel, used),
        shaped(f32, used + heads, LANES * rows),
        place,
        hidden,
        near,
        far,
        own,
        own_one,
        own_two,
        small_next,
        flops=4 * rows * depth * used,
        left=PLANES,
        scratch=[
            pltpu.VMEM((PLANES, used + heads, k_rows), bf16),
            pltpu.SemaphoreType.DMA((PLANES,)),
        ],
    )

    def early_products(backs, chunks, *totals):
        return call(
            functools.partial(early_kernel, backs),
            shaped(f32, LANES, rows, half),
            place,
            hidden,
            near,
            far,
            *totals,
            *chunks,
            flops=4 * rows * k_rows * half * len(backs),
        )

    early = early_products(
        ((0, True), (0, False), (1, True), (1, False)), (own, other, own_one, other_one)
    )
    early = early_products(((2, True),), (own_two,), early)
    share_other = send(share, swap)
    total = share + jnp.concatenate([share_other[:, rows:], share_other[:, :rows]], axis=1)
    some = total[:map_cols].astype(bf16)
    some_core = send(some, cores, "rep")
    some_chip = send(some, chips, "rep")
    some_both = send(some_chip, cores, "rep")
    mixing, loaded, c_rows, fac, meta = call(
        functools.partial(decay_kernel, map_cols),
        [
            shaped(bf16, LANES, mine, rows, rows),
            shaped(bf16, LANES, mine, NS, rows),
            shaped(bf16, LANES, rows, NS),
            shaped(f32, LANES, rows, 8),
            shaped(f32, 8, half),
        ],
        place,
        some,
        some_core,
        some_chip,
        some_both,
        total,
        dt_bias[:, None],
        decay_rate[:, None],
        flops=100 * mine * rows * rows,
    )
    inputs, ready, built = call(
        functools.partial(input_kernel, ((2, False),)),
        [
            shaped(bf16, LANES, rows, half),
            shaped(bf16, NS + 16, half),
            shaped(bf16, NS, half),
        ],
        place,
        hidden,
        near,
        far,
        early,
        from_next,
        other_two,
        loaded,
        meta,
        flops=rows * depth * half,
    )
    from_one = send(ready, shift(1, (0, 1, 2)))
    from_two = send(ready, shift(2, (0, 1)))
    local = call(
        local_kernel,
        shaped(f32, LANES, rows, half),
        place,
        inputs,
        mixing,
        skip[None],
        c_rows,
        built,
        fac,
        flops=4 * rows * rows * half,
    )

    def finish(partner):
        return call(
            functools.partial(final_kernel, partner, mine),
            shaped(bf16, rows, half),
            place,
            local,
            c_rows,
            fac,
            meta,
            from_one,
            from_two,
            flops=2 * rows * NS * half,
        )

    swapped = send(finish(True), swap)
    kept = finish(False)
    return pick(
        even,
        jnp.concatenate([kept, swapped], axis=1),
        jnp.concatenate([swapped, kept], axis=1),
    )


def shards(hidden, seg_ids, x_weight, bc_weight, dt_weight, dt_bias, decay_rate, skip):
    heads = dt_bias.shape[0]
    by_planes = (
        lax.axis_size("seq") == LANES * PLANES
        and lax.axis_size("rep") == 4
        and heads == SUBLANES
        and 2 * x_weight.shape[0] == x_weight.shape[1] == heads * P_SIZE
        and 2 * bc_weight.shape[1] == NS
        and hidden.shape[0] <= x_weight.shape[0]
        and 2 * LANES * hidden.shape[0] >= DOC_MAX
    )
    plan = plane_shards if by_planes else gathered_shards
    return plan(hidden, seg_ids, x_weight, bc_weight, dt_weight, dt_bias, decay_rate, skip)


def solution(mesh):
    placed = (
        P("seq", None),
        P("seq"),
        P("seq", "rep"),
        P("seq", "rep"),
        P("seq", "rep"),
        P("rep"),
        P("rep"),
        P("rep"),
    )
    return jax.shard_map(
        shards,
        mesh=mesh,
        in_specs=placed,
        out_specs=P("seq", "rep"),
        check_vma=False,
    )
```

```python
import functools
import math

import jax
import jax.numpy as jnp
from jax import lax
from jax.experimental import pallas as pl
from jax.experimental.pallas import tpu as pltpu
from jax.sharding import PartitionSpec as P

P_SIZE = 128
NS = 128
DOC_MAX = 1024
LANES = 2
PLANES = 4
SUBLANES = 8


def passed_along(x, axis, by):
    peers = lax.axis_size(axis)
    pairs = [(i, i + by) for i in range(peers) if 0 <= i + by < peers]
    return lax.ppermute(x, axis, pairs)


def state_read(c_block, state):
    upper_part = state.astype(jnp.bfloat16)
    lower_part = (state - upper_part.astype(jnp.float32)).astype(jnp.bfloat16)
    first = jnp.einsum("tn,hnp->thp", c_block, upper_part, preferred_element_type=jnp.float32)
    second = jnp.einsum("tn,hnp->thp", c_block, lower_part, preferred_element_type=jnp.float32)
    return first + second


def block_step(state, prev_seg, x_block, b_block, c_block, dt_block, rate_block, seg_block):
    count = x_block.shape[0]
    cum = jnp.cumsum(rate_block, axis=0)
    order = jnp.arange(count)
    masked = (order[:, None] >= order[None, :]) & (seg_block[:, None] == seg_block[None, :])
    scores = jnp.dot(c_block, b_block.T, preferred_element_type=jnp.float32)
    cum_heads = cum.T
    gaps = cum_heads[:, :, None] - cum_heads[:, None, :]
    decay = jnp.where(masked[None], jnp.exp(jnp.where(masked[None], gaps, 0.0)), 0.0)
    mixing = (scores[None] * decay * dt_block.T[:, None, :]).astype(jnp.bfloat16)
    diag_part = jnp.einsum("htj,jhp->thp", mixing, x_block, preferred_element_type=jnp.float32)
    keep = (seg_block == prev_seg).astype(jnp.float32)
    factor = jnp.exp(cum) * keep[:, None]
    carried = state_read(c_block, state) * factor[:, :, None]
    last_seg = seg_block[count - 1]
    tail = (
        jnp.exp(cum[count - 1][None, :] - cum)
        * dt_block
        * (seg_block == last_seg).astype(jnp.float32)[:, None]
    )
    loaded = (tail.T[:, :, None] * b_block.astype(jnp.float32)[None]).astype(jnp.bfloat16)
    built = jnp.einsum("hjn,jhp->hnp", loaded, x_block, preferred_element_type=jnp.float32)
    through = jnp.exp(cum[count - 1]) * (last_seg == prev_seg).astype(jnp.float32)
    new_state = built + through[:, None, None] * state
    return (diag_part + carried, new_state, last_seg)


def combine(earlier, later):
    early_state, early_keep, early_first, early_last = earlier
    late_state, late_keep, late_first, late_last = later
    linked = ((early_last == late_first) | (early_last < 0) | (late_first < 0)).astype(jnp.float32)
    passing = late_keep * linked
    return (
        late_state + passing[:, None, None] * early_state,
        early_keep * passing,
        jnp.where(early_first < 0, late_first, early_first),
        jnp.where(late_last < 0, early_last, late_last),
    )


def gathered_shards(hidden, seg_ids, x_weight, bc_weight, dt_weight, dt_bias, decay_rate, skip):
    tok_rows = hidden.shape[0]
    heads = dt_bias.shape[0]
    width = x_weight.shape[1]
    x_rows, bc_rows, dt_rows = (
        lax.all_gather(x_weight, "seq", axis=0, tiled=True),
        lax.all_gather(bc_weight, "seq", axis=0, tiled=True),
        lax.all_gather(dt_weight, "seq", axis=0, tiled=True),
    )
    x_total = jnp.dot(hidden, x_rows, preferred_element_type=jnp.float32)
    bc_total = jnp.dot(hidden, bc_rows, preferred_element_type=jnp.float32)
    dt_total = jnp.dot(hidden, dt_rows, preferred_element_type=jnp.float32)
    inputs = x_total.astype(jnp.bfloat16).reshape(tok_rows, heads, P_SIZE)
    maps = lax.all_gather(bc_total.astype(jnp.bfloat16), "rep", axis=1, tiled=True)
    b_all = maps[:, :NS]
    c_all = maps[:, NS:]
    steps = jax.nn.softplus(dt_total + dt_bias)
    rates = -steps * decay_rate
    state = jnp.zeros((heads, NS, P_SIZE), jnp.float32)
    prev_seg = jnp.int32(-1)
    result, state, prev_seg = block_step(
        state, prev_seg, inputs, b_all, c_all, steps, rates, seg_ids
    )
    whole_keep = jnp.exp(jnp.sum(rates, axis=0)) * (seg_ids[0] == seg_ids[tok_rows - 1]).astype(
        jnp.float32
    )
    element = (state, whole_keep, seg_ids[:1], seg_ids[tok_rows - 1 :])
    reach = DOC_MAX // tok_rows + 1
    first_hop = passed_along((element[0], element[1], element[2], element[3]), "seq", 1)
    incoming = first_hop
    for hop in range(reach - 1):
        incoming = combine(
            passed_along((incoming[0], incoming[1], incoming[2], incoming[3]), "seq", 1), first_hop
        )
    state_in = incoming[0]
    tag_in = incoming[3]
    running = jnp.cumsum(rates, axis=0)
    factor = jnp.exp(running) * (seg_ids == tag_in[0]).astype(jnp.float32)[:, None]
    extra = state_read(c_all, state_in) * factor[:, :, None]
    total_out = result + extra + skip[None, :, None] * inputs.astype(jnp.float32)
    return total_out.astype(jnp.bfloat16).reshape(tok_rows, width)


def pick(first, one, other):
    return jnp.where(first, one, other)


def call(body, outs, *operands, flops=0, scratch=(), left=0, grant=16):
    single = not isinstance(outs, list)
    shapes = [outs] if single else outs
    size = sum(math.prod(o.shape) * o.dtype.itemsize for o in (*operands, *shapes))
    result = pl.pallas_call(
        body,
        out_shape=shapes,
        in_specs=[pl.BlockSpec(memory_space=pltpu.SMEM)]
        + [pl.BlockSpec(memory_space=pltpu.VMEM)] * (len(operands) - 1 - left)
        + [pl.BlockSpec(memory_space=pl.ANY)] * left,
        out_specs=[pl.BlockSpec(memory_space=pltpu.VMEM)] * len(shapes),
        scratch_shapes=list(scratch),
        compiler_params=pltpu.CompilerParams(vmem_limit_bytes=grant * 2**20),
        cost_estimate=pl.CostEstimate(flops=flops, bytes_accessed=size, transcendentals=0),
    )(*operands)
    return result[0] if single else result


def contract_last(a, b):
    return lax.dot_general(a, b, (((1,), (1,)), ((), ())), preferred_element_type=jnp.float32)


def mul(a, b):
    return jnp.dot(a, b, preferred_element_type=jnp.float32)


def depth_blocks(place, token_refs, at, size):
    hidden_ref, near_ref, far_ref = token_refs
    own = hidden_ref[:, pl.ds(pl.multiple_of(at * size, size), size)]
    blocks = near_ref.shape[1] // size
    inside = pl.ds(pl.multiple_of((at % blocks) * size, size), size)
    is_near = (at // blocks) == place[2]
    return own, jnp.where(is_near, near_ref[:, inside], far_ref[:, inside])


def split_kernel(place, x_weight, bc, dt, ids, own, small, below, ids_in, done):
    f32, bf16 = jnp.float32, jnp.bfloat16
    lane = place[1]
    size, half = x_weight.shape[0], x_weight.shape[1] // 2
    maps, heads, rows = bc.shape[0], dt.shape[0], ids.shape[1]
    def columns(ref, index, width):
        return ref.at[:, pl.ds(pl.multiple_of(index * width, width), width)]

    moves = [
        (columns(x_weight, lane, half), own.at[pl.ds(0, size), :]),
        (bc, own.at[pl.ds(size, maps), :]),
        (bc, small.at[pl.ds(0, maps), :]),
        (dt, below),
        (ids, ids_in),
    ]
    copies = [pltpu.make_async_copy(a, b, done.at[i]) for i, (a, b) in enumerate(moves)]
    for copy in copies:
        copy.start()
    for copy in copies:
        copy.wait()
    row = lax.broadcasted_iota(jnp.int32, (heads, rows), 0)
    notes = jnp.where(row == 0, ids_in[...].astype(f32), 0.0)
    notes = jnp.concatenate([notes, jnp.zeros((heads, size - rows), f32)], axis=1)
    last = jnp.concatenate([below[...].astype(f32), notes], axis=0).astype(bf16)
    own[size + maps :, :] = last
    small[maps:, :] = last


def share_kernel(used, place, hidden, near, far, c0, c1, c2, s3, out, small, done):
    plane, lane = place[0], place[1]
    rows = hidden.shape[0]
    size = c0.shape[1]
    below = pl.ds(size, c0.shape[0] - size)
    copies = [
        pltpu.make_async_copy(c.at[below, :], small.at[i], done.at[i])
        for i, c in enumerate((c0, c1, c2))
    ]
    copies.append(pltpu.make_async_copy(s3, small.at[3], done.at[3]))
    for copy in copies:
        copy.start()
    totals = [None, None]
    for back, copy in enumerate(copies):
        at = LANES * ((plane + PLANES - back) % PLANES) + lane
        copy.wait()
        weights = small[back]
        for r, tokens in enumerate(depth_blocks(place, (hidden, near, far), at, size)):
            product = contract_last(weights, tokens)
            totals[r] = product if totals[r] is None else totals[r] + product
    notes = [small[i, used:, :rows].astype(jnp.float32) for i in range(3)]
    row = lax.broadcasted_iota(jnp.int32, notes[0].shape, 0)
    ends = [n[0:1, rows - 1 : rows] for n in notes[1:]]
    note = jnp.where(row == 1, ends[0], jnp.where(row == 2, ends[1], notes[0]))
    out[:used, :rows] = totals[0][:used]
    out[:used, rows:] = totals[1][:used]
    out[used:, :rows] = note
    out[used:, rows:] = jnp.zeros_like(note)


def decay_kernel(
    map_cols, place, some, some_core, some_chip, some_both, total, bias, rate_of, mixing, loaded, c_out, fac, meta
):
    f32, bf16 = jnp.float32, jnp.bfloat16
    plane, lane = place[0], place[1]
    first_core, first_chip = place[2] == 0, place[3] == 0
    here = [pick(first_core, a[...], b[...]) for a, b in ((some, some_core), (some_core, some))]
    there = [
        pick(first_core, a[...], b[...])
        for a, b in ((some_chip, some_both), (some_both, some_chip))
    ]
    here, there = jnp.concatenate(here, axis=0), jnp.concatenate(there, axis=0)
    b_maps, c_maps = pick(first_chip, here, there), pick(first_chip, there, here)
    heads = bias.shape[0]
    mine = heads // 2
    rows = total.shape[1] // 2
    even = lane == 0
    pre = total[map_cols : map_cols + heads, :] + bias[...]
    steps = jnp.maximum(pre, 0.0) + jnp.log1p(jnp.exp(-jnp.abs(pre)))
    rates = -steps * rate_of[...]
    steps = jnp.where(even, steps[:mine], steps[mine:])
    rates = jnp.where(even, rates[:mine], rates[mine:])
    notes = total[map_cols + heads :, :]
    tri_row = lax.broadcasted_iota(jnp.int32, (rows, rows), 0)
    tri_col = lax.broadcasted_iota(jnp.int32, (rows, rows), 1)
    upper = (tri_row <= tri_col).astype(f32)
    causal = tri_row >= tri_col
    pad = jnp.zeros((8 - mine, rows), f32)
    cums, lasts = [], []
    for r in range(2):
        cut = slice(r * rows, (r + 1) * rows)
        cums.append(
            lax.dot_general(
                jnp.concatenate([rates[:, cut], pad], axis=0),
                upper,
                (((1,), (0,)), ((), ())),
                precision=lax.Precision.HIGHEST,
                preferred_element_type=f32,
            )
        )
        lasts.append(notes[0:1, (r + 1) * rows - 1 : (r + 1) * rows])
    end = [c[:mine, rows - 1 : rows] for c in cums]
    end0, end1 = pick(even, end[0], end[1]), pick(even, end[1], end[0])
    last0, last1 = pick(even, lasts[0], lasts[1]), pick(even, lasts[1], lasts[0])
    final = pick(even, notes[:, 2 * rows - 1 :], notes[:, rows - 1 : rows])
    tag = jnp.where(plane > 0, final[1:2], -1.0)
    tag_before = jnp.where(plane > 1, final[2:3], -1.0)
    link = jnp.exp(end1) * (last1 == last0).astype(f32)
    enters = jnp.exp(end0) * (last0 == tag).astype(f32)
    through = jnp.exp(end0 + end1)
    passes = (tag == tag_before).astype(f32)
    width = meta.shape[1] // mine
    meta[...] = jnp.zeros_like(meta)
    for h in range(mine):
        cut = slice(h * width, (h + 1) * width)
        meta[0:1, cut] = jnp.broadcast_to(link[h : h + 1], (1, width))
        meta[1:2, cut] = jnp.broadcast_to(enters[h : h + 1], (1, width))
        meta[2:3, cut] = jnp.broadcast_to(through[h : h + 1], (1, width))
        meta[3:4, cut] = jnp.broadcast_to(passes, (1, width))
    for r in range(2):
        b = lane if r == 0 else 1 - lane
        cut = slice(r * rows, (r + 1) * rows)
        seg, cum, dt = notes[0:1, cut], cums[r], steps[:, cut]
        source = jnp.where(b == 0, tag, last0)
        factor = jnp.exp(cum) * (seg == source).astype(f32)
        fac[b] = factor.T
        cols = jnp.concatenate([cum[:mine], jnp.broadcast_to(seg, (8 - mine, rows))], axis=0).T
        keep = causal & (cols[:, mine : mine + 1] == seg)
        b_t, c_t = b_maps[:, cut], c_maps[:, cut]
        c_rows = c_t.astype(f32).T.astype(bf16)
        c_out[b] = c_rows
        scores = mul(c_rows, b_t)
        tail = jnp.exp(end[r] - cum[:mine]) * dt * (seg == lasts[r]).astype(f32)
        wide = b_t.astype(f32)
        for h in range(mine):
            gap = cols[:, h : h + 1] - cum[h : h + 1]
            decay = jnp.where(keep, jnp.exp(jnp.where(keep, gap, 0.0)), 0.0)
            mixing[b, h] = (scores * decay * dt[h : h + 1]).astype(bf16)
            loaded[b, h] = (wide * tail[h : h + 1]).astype(bf16)


def add_products(place, token_refs, backs, weight_refs, totals):
    plane, lane = place[0], place[1]
    for (back, is_own), w in zip(backs, weight_refs):
        at = LANES * ((plane + PLANES - back) % PLANES) + (lane if is_own else 1 - lane)
        size = w.shape[1]
        weights = w[:size, :]
        for r, tokens in enumerate(depth_blocks(place, token_refs, at, size)):
            product = mul(tokens, weights)
            totals[r] = product if totals[r] is None else totals[r] + product


def early_kernel(backs, place, hidden, near, far, *refs):
    *weights, out = refs
    totals = [None, None]
    if len(weights) > len(backs):
        totals = [weights[0][0], weights[0][1]]
        weights = weights[1:]
    add_products(place, (hidden, near, far), backs, weights, totals)
    out[0] = totals[0]
    out[1] = totals[1]


def neighbour_kernel(place, mine, far, own, other, out):
    same = place[1] == place[2]
    size = other.shape[0]
    here, there = mine[...], far[...]
    first, second = jnp.where(same, here, there), jnp.where(same, there, here)
    out[...] = (mul(first, own[:size, :]) + mul(second, other[...])).astype(out.dtype)


def input_kernel(backs, place, hidden, near, far, acc, back, *refs):
    *chunks, loaded, meta, x_out, ready, built_out = refs
    f32, bf16 = jnp.float32, jnp.bfloat16
    lane = place[1]
    rows = hidden.shape[0]
    totals = [acc[0] + back[:rows, :].astype(f32), acc[1] + back[rows : 2 * rows, :].astype(f32)]
    add_products(place, (hidden, near, far), backs, chunks, totals)
    x_out[lane] = totals[0].astype(bf16)
    x_out[1 - lane] = totals[1].astype(bf16)
    mine = loaded.shape[1]
    width = meta.shape[1] // mine
    for h in range(mine):
        cut = slice(h * width, (h + 1) * width)
        first = mul(loaded[0, h], x_out[0, :, cut])
        second = mul(loaded[1, h], x_out[1, :, cut])
        ready[:NS, cut] = (second + meta[0:1, cut] * first).astype(bf16)
        built_out[:, cut] = first.astype(bf16)
    through = meta[2:3, :]
    upper = through.astype(bf16)
    lower = (through - upper.astype(f32)).astype(bf16)
    row = lax.broadcasted_iota(jnp.int32, (ready.shape[0] - NS, ready.shape[1]), 0)
    ready[NS:, :] = jnp.where(
        row == 0, upper.astype(f32), jnp.where(row == 1, lower.astype(f32), 0.0)
    ).astype(bf16)


def local_kernel(place, x, mixing, skip, c_rows, built, fac, out):
    lane = place[1]
    mine = mixing.shape[1]
    width = x.shape[2] // mine
    carried = mul(c_rows[1], built[...])
    gains = jnp.where(lane == 0, skip[:, :mine], skip[:, mine:])
    for h in range(mine):
        cut = slice(h * width, (h + 1) * width)
        for b in range(2):
            xs = x[b, :, cut]
            local = mul(mixing[b, h], xs) + gains[:, h : h + 1] * xs.astype(jnp.float32)
            if b == 1:
                local = local + fac[1, :, h : h + 1] * carried[:, cut]
            out[b, :, cut] = local


def final_kernel(partner, mine, place, local, c_rows, fac, meta, one, two, out):
    f32, bf16 = jnp.float32, jnp.bfloat16
    lane = place[1]
    b = 1 - lane if partner else lane
    through = one[NS : NS + 1, :].astype(f32) + one[NS + 1 : NS + 2, :].astype(f32)
    incoming = one[:NS, :].astype(f32) + (through * meta[3:4, :]) * two[:NS, :].astype(f32)
    entering = (incoming * jnp.where(b == 1, meta[1:2, :], 1.0)).astype(bf16)
    carried = mul(c_rows[b], entering)
    factor = fac[b]
    width = out.shape[1] // mine
    for h in range(mine):
        cut = slice(h * width, (h + 1) * width)
        out[:, cut] = (local[b, :, cut] + factor[:, h : h + 1] * carried[:, cut]).astype(bf16)


def plane_shards(hidden, seg_ids, x_weight, bc_weight, dt_weight, dt_bias, decay_rate, skip):
    bf16, f32 = jnp.bfloat16, jnp.float32
    me = lax.axis_index("seq")
    lane, plane = me % LANES, me // LANES
    even = lane == 0
    core = lax.axis_index("rep") % 2
    place = jnp.stack([plane, lane, core, lax.axis_index("rep") // 2]).astype(jnp.int32)
    rows, depth = hidden.shape
    k_rows, cols = x_weight.shape
    half = cols // 2
    heads = dt_bias.shape[0]
    mine = heads // 2
    map_cols = bc_weight.shape[1]
    used = map_cols + heads

    def shaped(dtype, *shape):
        return jax.ShapeDtypeStruct(shape, dtype)

    def at(p, l):
        return LANES * p + l

    swap = [(i, i ^ 1) for i in range(LANES * PLANES)]
    cores = [(i, i ^ 1) for i in range(lax.axis_size("rep"))]
    chips = [(i, i ^ 2) for i in range(lax.axis_size("rep"))]

    def shift(by, sources):
        return [(at(p, l), at(p + by, l)) for p in sources for l in range(LANES)]

    along = [(at(p, l), at((p + 1) % PLANES, l)) for p in range(PLANES) for l in range(LANES)]
    back = [(b, a) for a, b in along]

    def send(x, pairs, axis="seq"):
        return lax.ppermute(x, axis, pairs)

    together = lax.optimization_barrier

    ahead_at = (LANES * ((plane + 1) % PLANES) + core) * k_rows
    ahead = send(lax.dynamic_slice_in_dim(hidden, ahead_at, k_rows, 1), along)
    sent = lax.dynamic_slice_in_dim(x_weight, (1 - lane) * half, half, 1)
    other = send(sent, swap)
    own, small = call(
        split_kernel,
        [
            shaped(bf16, k_rows + used + heads, half),
            shaped(bf16, used + heads, k_rows),
        ],
        place,
        x_weight,
        bc_weight.T,
        dt_weight.T,
        seg_ids[None],
        left=4,
        grant=60,
        scratch=[
            pltpu.VMEM((heads, k_rows), bf16),
            pltpu.VMEM((1, rows), jnp.int32),
            pltpu.SemaphoreType.DMA((5,)),
        ],
    )
    own_one = send(own, along)
    small_next = send(small, back)
    near = pick(core == 0, hidden[:, : depth // 2], hidden[:, depth // 2 :])
    ahead_other = send(ahead, swap)
    other, own_one, ahead, ahead_other = together((other, own_one, ahead, ahead_other))

    other_one = send(other, along)
    own_two = send(own_one, along)
    near = send(near, swap)
    ahead = jnp.concatenate([ahead, ahead_other], axis=0)
    ahead_far = send(ahead, cores, "rep")
    part = call(
        neighbour_kernel,
        shaped(bf16, LANES * rows, half),
        place,
        ahead,
        ahead_far,
        own,
        other,
        flops=4 * rows * LANES * k_rows * half,
    )
    other_one, own_two, near, part = together((other_one, own_two, near, part))

    other_two = send(other_one, along)
    from_next = send(part, back)
    far = send(near, cores, "rep")
    share = call(
        functools.partial(share_kernel, used),
        shaped(f32, used + heads, LANES * rows),
        place,
        hidden,
        near,
        far,
        own,
        own_one,
        own_two,
        small_next,
        flops=4 * rows * depth * used,
        left=PLANES,
        scratch=[
            pltpu.VMEM((PLANES, used + heads, k_rows), bf16),
            pltpu.SemaphoreType.DMA((PLANES,)),
        ],
    )

    def early_products(backs, chunks, *totals):
        return call(
            functools.partial(early_kernel, backs),
            shaped(f32, LANES, rows, half),
            place,
            hidden,
            near,
            far,
            *totals,
            *chunks,
            flops=4 * rows * k_rows * half * len(backs),
        )

    early = early_products(
        ((0, True), (0, False), (1, True), (1, False)), (own, other, own_one, other_one)
    )
    early = early_products(((2, True),), (own_two,), early)
    share_other = send(share, swap)
    total = share + jnp.concatenate([share_other[:, rows:], share_other[:, :rows]], axis=1)
    some = total[:map_cols].astype(bf16)
    some_core = send(some, cores, "rep")
    some_chip = send(some, chips, "rep")
    some_both = send(some_chip, cores, "rep")
    mixing, loaded, c_rows, fac, meta = call(
        functools.partial(decay_kernel, map_cols),
        [
            shaped(bf16, LANES, mine, rows, rows),
            shaped(bf16, LANES, mine, NS, rows),
            shaped(bf16, LANES, rows, NS),
            shaped(f32, LANES, rows, 8),
            shaped(f32, 8, half),
        ],
        place,
        some,
        some_core,
        some_chip,
        some_both,
        total,
        dt_bias[:, None],
        decay_rate[:, None],
        flops=100 * mine * rows * rows,
    )
    inputs, ready, built = call(
        functools.partial(input_kernel, ((2, False),)),
        [
            shaped(bf16, LANES, rows, half),
            shaped(bf16, NS + 16, half),
            shaped(bf16, NS, half),
        ],
        place,
        hidden,
        near,
        far,
        early,
        from_next,
        other_two,
        loaded,
        meta,
        flops=rows * depth * half,
    )
    from_one = send(ready, shift(1, (0, 1, 2)))
    from_two = send(ready, shift(2, (0, 1)))
    local = call(
        local_kernel,
        shaped(f32, LANES, rows, half),
        place,
        inputs,
        mixing,
        skip[None],
        c_rows,
        built,
        fac,
        flops=4 * rows * rows * half,
    )

    def finish(partner):
        return call(
            functools.partial(final_kernel, partner, mine),
            shaped(bf16, rows, half),
            place,
            local,
            c_rows,
            fac,
            meta,
            from_one,
            from_two,
            flops=2 * rows * NS * half,
        )

    swapped = send(finish(True), swap)
    kept = finish(False)
    return pick(
        even,
        jnp.concatenate([kept, swapped], axis=1),
        jnp.concatenate([swapped, kept], axis=1),
    )


def shards(hidden, seg_ids, x_weight, bc_weight, dt_weight, dt_bias, decay_rate, skip):
    heads = dt_bias.shape[0]
    by_planes = (
        lax.axis_size("seq") == LANES * PLANES
        and lax.axis_size("rep") == 4
        and heads == SUBLANES
        and 2 * x_weight.shape[0] == x_weight.shape[1] == heads * P_SIZE
        and 2 * bc_weight.shape[1] == NS
        and hidden.shape[0] <= x_weight.shape[0]
        and 2 * LANES * hidden.shape[0] >= DOC_MAX
    )
    plan = plane_shards if by_planes else gathered_shards
    return plan(hidden, seg_ids, x_weight, bc_weight, dt_weight, dt_bias, decay_rate, skip)


def solution(mesh):
    placed = (
        P("seq", None),
        P("seq"),
        P("seq", "rep"),
        P("seq", "rep"),
        P("seq", "rep"),
        P("rep"),
        P("rep"),
        P("rep"),
    )
    return jax.shard_map(
        shards,
        mesh=mesh,
        in_specs=placed,
        out_specs=P("seq", "rep"),
        check_vma=False,
    )
```

```python
import functools
import math

import jax
import jax.numpy as jnp
from jax import lax
from jax.experimental import pallas as pl
from jax.experimental.pallas import tpu as pltpu
from jax.sharding import PartitionSpec as P

P_SIZE = 128
NS = 128
DOC_MAX = 1024
LANES = 2
PLANES = 4
SUBLANES = 8


def passed_along(x, axis, by):
    peers = lax.axis_size(axis)
    pairs = [(i, i + by) for i in range(peers) if 0 <= i + by < peers]
    return lax.ppermute(x, axis, pairs)


def state_read(c_block, state):
    upper_part = state.astype(jnp.bfloat16)
    lower_part = (state - upper_part.astype(jnp.float32)).astype(jnp.bfloat16)
    first = jnp.einsum("tn,hnp->thp", c_block, upper_part, preferred_element_type=jnp.float32)
    second = jnp.einsum("tn,hnp->thp", c_block, lower_part, preferred_element_type=jnp.float32)
    return first + second


def block_step(state, prev_seg, x_block, b_block, c_block, dt_block, rate_block, seg_block):
    count = x_block.shape[0]
    cum = jnp.cumsum(rate_block, axis=0)
    order = jnp.arange(count)
    masked = (order[:, None] >= order[None, :]) & (seg_block[:, None] == seg_block[None, :])
    scores = jnp.dot(c_block, b_block.T, preferred_element_type=jnp.float32)
    cum_heads = cum.T
    gaps = cum_heads[:, :, None] - cum_heads[:, None, :]
    decay = jnp.where(masked[None], jnp.exp(jnp.where(masked[None], gaps, 0.0)), 0.0)
    mixing = (scores[None] * decay * dt_block.T[:, None, :]).astype(jnp.bfloat16)
    diag_part = jnp.einsum("htj,jhp->thp", mixing, x_block, preferred_element_type=jnp.float32)
    keep = (seg_block == prev_seg).astype(jnp.float32)
    factor = jnp.exp(cum) * keep[:, None]
    carried = state_read(c_block, state) * factor[:, :, None]
    last_seg = seg_block[count - 1]
    tail = (
        jnp.exp(cum[count - 1][None, :] - cum)
        * dt_block
        * (seg_block == last_seg).astype(jnp.float32)[:, None]
    )
    loaded = (tail.T[:, :, None] * b_block.astype(jnp.float32)[None]).astype(jnp.bfloat16)
    built = jnp.einsum("hjn,jhp->hnp", loaded, x_block, preferred_element_type=jnp.float32)
    through = jnp.exp(cum[count - 1]) * (last_seg == prev_seg).astype(jnp.float32)
    new_state = built + through[:, None, None] * state
    return (diag_part + carried, new_state, last_seg)


def combine(earlier, later):
    early_state, early_keep, early_first, early_last = earlier
    late_state, late_keep, late_first, late_last = later
    linked = ((early_last == late_first) | (early_last < 0) | (late_first < 0)).astype(jnp.float32)
    passing = late_keep * linked
    return (
        late_state + passing[:, None, None] * early_state,
        early_keep * passing,
        jnp.where(early_first < 0, late_first, early_first),
        jnp.where(late_last < 0, early_last, late_last),
    )


def gathered_shards(hidden, seg_ids, x_weight, bc_weight, dt_weight, dt_bias, decay_rate, skip):
    tok_rows = hidden.shape[0]
    heads = dt_bias.shape[0]
    width = x_weight.shape[1]
    x_rows, bc_rows, dt_rows = (
        lax.all_gather(x_weight, "seq", axis=0, tiled=True),
        lax.all_gather(bc_weight, "seq", axis=0, tiled=True),
        lax.all_gather(dt_weight, "seq", axis=0, tiled=True),
    )
    x_total = jnp.dot(hidden, x_rows, preferred_element_type=jnp.float32)
    bc_total = jnp.dot(hidden, bc_rows, preferred_element_type=jnp.float32)
    dt_total = jnp.dot(hidden, dt_rows, preferred_element_type=jnp.float32)
    inputs = x_total.astype(jnp.bfloat16).reshape(tok_rows, heads, P_SIZE)
    maps = lax.all_gather(bc_total.astype(jnp.bfloat16), "rep", axis=1, tiled=True)
    b_all = maps[:, :NS]
    c_all = maps[:, NS:]
    steps = jax.nn.softplus(dt_total + dt_bias)
    rates = -steps * decay_rate
    state = jnp.zeros((heads, NS, P_SIZE), jnp.float32)
    prev_seg = jnp.int32(-1)
    result, state, prev_seg = block_step(
        state, prev_seg, inputs, b_all, c_all, steps, rates, seg_ids
    )
    whole_keep = jnp.exp(jnp.sum(rates, axis=0)) * (seg_ids[0] == seg_ids[tok_rows - 1]).astype(
        jnp.float32
    )
    element = (state, whole_keep, seg_ids[:1], seg_ids[tok_rows - 1 :])
    reach = DOC_MAX // tok_rows + 1
    first_hop = passed_along((element[0], element[1], element[2], element[3]), "seq", 1)
    incoming = first_hop
    for hop in range(reach - 1):
        incoming = combine(
            passed_along((incoming[0], incoming[1], incoming[2], incoming[3]), "seq", 1), first_hop
        )
    state_in = incoming[0]
    tag_in = incoming[3]
    running = jnp.cumsum(rates, axis=0)
    factor = jnp.exp(running) * (seg_ids == tag_in[0]).astype(jnp.float32)[:, None]
    extra = state_read(c_all, state_in) * factor[:, :, None]
    total_out = result + extra + skip[None, :, None] * inputs.astype(jnp.float32)
    return total_out.astype(jnp.bfloat16).reshape(tok_rows, width)


def pick(first, one, other):
    return jnp.where(first, one, other)


def call(body, outs, *operands, flops=0, scratch=(), left=0, grant=16):
    single = not isinstance(outs, list)
    shapes = [outs] if single else outs
    size = sum(math.prod(o.shape) * o.dtype.itemsize for o in (*operands, *shapes))
    result = pl.pallas_call(
        body,
        out_shape=shapes,
        in_specs=[pl.BlockSpec(memory_space=pltpu.SMEM)]
        + [pl.BlockSpec(memory_space=pltpu.VMEM)] * (len(operands) - 1 - left)
        + [pl.BlockSpec(memory_space=pl.ANY)] * left,
        out_specs=[pl.BlockSpec(memory_space=pltpu.VMEM)] * len(shapes),
        scratch_shapes=list(scratch),
        compiler_params=pltpu.CompilerParams(vmem_limit_bytes=grant * 2**20),
        cost_estimate=pl.CostEstimate(flops=flops, bytes_accessed=size, transcendentals=0),
    )(*operands)
    return result[0] if single else result


def contract_last(a, b):
    return lax.dot_general(a, b, (((1,), (1,)), ((), ())), preferred_element_type=jnp.float32)


def mul(a, b):
    return jnp.dot(a, b, preferred_element_type=jnp.float32)


def depth_blocks(place, token_refs, at, size):
    hidden_ref, near_ref, far_ref = token_refs
    own = hidden_ref[:, pl.ds(pl.multiple_of(at * size, size), size)]
    blocks = near_ref.shape[1] // size
    inside = pl.ds(pl.multiple_of((at % blocks) * size, size), size)
    is_near = (at // blocks) == place[2]
    return own, jnp.where(is_near, near_ref[:, inside], far_ref[:, inside])


def split_kernel(place, x_weight, bc, dt, ids, own, small, below, ids_in, done):
    f32, bf16 = jnp.float32, jnp.bfloat16
    lane = place[1]
    size, half = x_weight.shape[0], x_weight.shape[1] // 2
    maps, heads, rows = bc.shape[0], dt.shape[0], ids.shape[1]
    def columns(ref, index, width):
        return ref.at[:, pl.ds(pl.multiple_of(index * width, width), width)]

    moves = [
        (columns(x_weight, lane, half), own.at[pl.ds(0, size), :]),
        (bc, own.at[pl.ds(size, maps), :]),
        (bc, small.at[pl.ds(0, maps), :]),
        (dt, below),
        (ids, ids_in),
    ]
    copies = [pltpu.make_async_copy(a, b, done.at[i]) for i, (a, b) in enumerate(moves)]
    for copy in copies:
        copy.start()
    for copy in copies:
        copy.wait()
    row = lax.broadcasted_iota(jnp.int32, (heads, rows), 0)
    notes = jnp.where(row == 0, ids_in[...].astype(f32), 0.0)
    notes = jnp.concatenate([notes, jnp.zeros((heads, size - rows), f32)], axis=1)
    last = jnp.concatenate([below[...].astype(f32), notes], axis=0).astype(bf16)
    own[size + maps :, :] = last
    small[maps:, :] = last


def share_kernel(used, place, hidden, near, far, c0, c1, c2, s3, out, small, done):
    plane, lane = place[0], place[1]
    rows = hidden.shape[0]
    size = c0.shape[1]
    below = pl.ds(size, c0.shape[0] - size)
    copies = [
        pltpu.make_async_copy(c.at[below, :], small.at[i], done.at[i])
        for i, c in enumerate((c0, c1, c2))
    ]
    copies.append(pltpu.make_async_copy(s3, small.at[3], done.at[3]))
    for copy in copies:
        copy.start()
    totals = [None, None]
    for back, copy in enumerate(copies):
        at = LANES * ((plane + PLANES - back) % PLANES) + lane
        copy.wait()
        weights = small[back]
        for r, tokens in enumerate(depth_blocks(place, (hidden, near, far), at, size)):
            product = contract_last(weights, tokens)
            totals[r] = product if totals[r] is None else totals[r] + product
    notes = [small[i, used:, :rows].astype(jnp.float32) for i in range(3)]
    row = lax.broadcasted_iota(jnp.int32, notes[0].shape, 0)
    ends = [n[0:1, rows - 1 : rows] for n in notes[1:]]
    note = jnp.where(row == 1, ends[0], jnp.where(row == 2, ends[1], notes[0]))
    out[:used, :rows] = totals[0][:used]
    out[:used, rows:] = totals[1][:used]
    out[used:, :rows] = note
    out[used:, rows:] = jnp.zeros_like(note)


def decay_kernel(
    map_cols, place, some, some_core, some_chip, some_both, total, bias, rate_of, mixing, loaded, c_out, fac, meta, passing
):
    f32, bf16 = jnp.float32, jnp.bfloat16
    plane, lane = place[0], place[1]
    first_core, first_chip = place[2] == 0, place[3] == 0
    here = [pick(first_core, a[...], b[...]) for a, b in ((some, some_core), (some_core, some))]
    there = [
        pick(first_core, a[...], b[...])
        for a, b in ((some_chip, some_both), (some_both, some_chip))
    ]
    here, there = jnp.concatenate(here, axis=0), jnp.concatenate(there, axis=0)
    b_maps, c_maps = pick(first_chip, here, there), pick(first_chip, there, here)
    heads = bias.shape[0]
    mine = heads // 2
    rows = total.shape[1] // 2
    even = lane == 0
    pre = total[map_cols : map_cols + heads, :] + bias[...]
    steps = jnp.maximum(pre, 0.0) + jnp.log1p(jnp.exp(-jnp.abs(pre)))
    rates = -steps * rate_of[...]
    steps = jnp.where(even, steps[:mine], steps[mine:])
    rates = jnp.where(even, rates[:mine], rates[mine:])
    notes = total[map_cols + heads :, :]
    tri_row = lax.broadcasted_iota(jnp.int32, (rows, rows), 0)
    tri_col = lax.broadcasted_iota(jnp.int32, (rows, rows), 1)
    upper = (tri_row <= tri_col).astype(f32)
    causal = tri_row >= tri_col
    pad = jnp.zeros((8 - mine, rows), f32)
    cums, lasts = [], []
    for r in range(2):
        cut = slice(r * rows, (r + 1) * rows)
        cums.append(
            lax.dot_general(
                jnp.concatenate([rates[:, cut], pad], axis=0),
                upper,
                (((1,), (0,)), ((), ())),
                precision=lax.Precision.HIGHEST,
                preferred_element_type=f32,
            )
        )
        lasts.append(notes[0:1, (r + 1) * rows - 1 : (r + 1) * rows])
    end = [c[:mine, rows - 1 : rows] for c in cums]
    end0, end1 = pick(even, end[0], end[1]), pick(even, end[1], end[0])
    last0, last1 = pick(even, lasts[0], lasts[1]), pick(even, lasts[1], lasts[0])
    final = pick(even, notes[:, 2 * rows - 1 :], notes[:, rows - 1 : rows])
    tag = jnp.where(plane > 0, final[1:2], -1.0)
    tag_before = jnp.where(plane > 1, final[2:3], -1.0)
    link = jnp.exp(end1) * (last1 == last0).astype(f32)
    enters = jnp.exp(end0) * (last0 == tag).astype(f32)
    through = jnp.exp(end0 + end1)
    passes = (tag == tag_before).astype(f32)
    width = meta.shape[1] // mine
    meta[...] = jnp.zeros_like(meta)
    for h in range(mine):
        cut = slice(h * width, (h + 1) * width)
        meta[0:1, cut] = jnp.broadcast_to(link[h : h + 1], (1, width))
        meta[1:2, cut] = jnp.broadcast_to(enters[h : h + 1], (1, width))
        meta[2:3, cut] = jnp.broadcast_to(through[h : h + 1], (1, width))
        meta[3:4, cut] = jnp.broadcast_to(passes, (1, width))
    whole = meta[2:3, :]
    upper_part = whole.astype(bf16).astype(f32)
    row = lax.broadcasted_iota(jnp.int32, passing.shape, 0)
    passing[...] = jnp.where(
        row == 0, upper_part, jnp.where(row == 1, whole - upper_part, 0.0)
    ).astype(bf16)
    for r in range(2):
        b = lane if r == 0 else 1 - lane
        cut = slice(r * rows, (r + 1) * rows)
        seg, cum, dt = notes[0:1, cut], cums[r], steps[:, cut]
        source = jnp.where(b == 0, tag, last0)
        factor = jnp.exp(cum) * (seg == source).astype(f32)
        fac[b] = factor.T
        cols = jnp.concatenate([cum[:mine], jnp.broadcast_to(seg, (8 - mine, rows))], axis=0).T
        keep = causal & (cols[:, mine : mine + 1] == seg)
        b_t, c_t = b_maps[:, cut], c_maps[:, cut]
        c_rows = c_t.astype(f32).T.astype(bf16)
        c_out[b] = c_rows
        scores = mul(c_rows, b_t)
        tail = jnp.exp(end[r] - cum[:mine]) * dt * (seg == lasts[r]).astype(f32)
        wide = b_t.astype(f32)
        for h in range(mine):
            gap = cols[:, h : h + 1] - cum[h : h + 1]
            decay = jnp.where(keep, jnp.exp(jnp.where(keep, gap, 0.0)), 0.0)
            mixing[b, h] = (scores * decay * dt[h : h + 1]).astype(bf16)
            loaded[b, h] = (wide * tail[h : h + 1]).astype(bf16)


def add_products(place, token_refs, backs, weight_refs, totals):
    plane, lane = place[0], place[1]
    for (back, is_own), w in zip(backs, weight_refs):
        at = LANES * ((plane + PLANES - back) % PLANES) + (lane if is_own else 1 - lane)
        size = w.shape[1]
        weights = w[:size, :]
        for r, tokens in enumerate(depth_blocks(place, token_refs, at, size)):
            product = mul(tokens, weights)
            totals[r] = product if totals[r] is None else totals[r] + product


def early_kernel(backs, place, hidden, near, far, *refs):
    *weights, out = refs
    totals = [None, None]
    if len(weights) > len(backs):
        totals = [weights[0][0], weights[0][1]]
        weights = weights[1:]
    add_products(place, (hidden, near, far), backs, weights, totals)
    out[0] = totals[0]
    out[1] = totals[1]


def neighbour_kernel(place, mine, far, own, other, out):
    same = place[1] == place[2]
    size = other.shape[0]
    here, there = mine[...], far[...]
    first, second = jnp.where(same, here, there), jnp.where(same, there, here)
    out[...] = (mul(first, own[:size, :]) + mul(second, other[...])).astype(out.dtype)


def input_kernel(backs, place, hidden, near, far, acc, back, *refs):
    *chunks, loaded, meta, x_out, ready, built_out = refs
    f32, bf16 = jnp.float32, jnp.bfloat16
    lane = place[1]
    rows = hidden.shape[0]
    totals = [acc[0] + back[:rows, :].astype(f32), acc[1] + back[rows : 2 * rows, :].astype(f32)]
    add_products(place, (hidden, near, far), backs, chunks, totals)
    x_out[lane] = totals[0].astype(bf16)
    x_out[1 - lane] = totals[1].astype(bf16)
    mine = loaded.shape[1]
    width = meta.shape[1] // mine
    for h in range(mine):
        cut = slice(h * width, (h + 1) * width)
        first = mul(loaded[0, h], x_out[0, :, cut])
        second = mul(loaded[1, h], x_out[1, :, cut])
        ready[:, cut] = (second + meta[0:1, cut] * first).astype(bf16)
        built_out[:, cut] = first.astype(bf16)


def local_kernel(place, x, mixing, skip, c_rows, built, fac, out):
    lane = place[1]
    mine = mixing.shape[1]
    width = x.shape[2] // mine
    carried = mul(c_rows[1], built[...])
    gains = jnp.where(lane == 0, skip[:, :mine], skip[:, mine:])
    for h in range(mine):
        cut = slice(h * width, (h + 1) * width)
        for b in range(2):
            xs = x[b, :, cut]
            local = mul(mixing[b, h], xs) + gains[:, h : h + 1] * xs.astype(jnp.float32)
            if b == 1:
                local = local + fac[1, :, h : h + 1] * carried[:, cut]
            out[b, :, cut] = local


def final_kernel(partner, mine, place, local, c_rows, fac, meta, passed, one, two, out):
    f32, bf16 = jnp.float32, jnp.bfloat16
    lane = place[1]
    b = 1 - lane if partner else lane
    through = passed[0:1, :].astype(f32) + passed[1:2, :].astype(f32)
    incoming = one[...].astype(f32) + (through * meta[3:4, :]) * two[...].astype(f32)
    entering = (incoming * jnp.where(b == 1, meta[1:2, :], 1.0)).astype(bf16)
    carried = mul(c_rows[b], entering)
    factor = fac[b]
    width = out.shape[1] // mine
    for h in range(mine):
        cut = slice(h * width, (h + 1) * width)
        out[:, cut] = (local[b, :, cut] + factor[:, h : h + 1] * carried[:, cut]).astype(bf16)


def plane_shards(hidden, seg_ids, x_weight, bc_weight, dt_weight, dt_bias, decay_rate, skip):
    bf16, f32 = jnp.bfloat16, jnp.float32
    me = lax.axis_index("seq")
    lane, plane = me % LANES, me // LANES
    even = lane == 0
    core = lax.axis_index("rep") % 2
    place = jnp.stack([plane, lane, core, lax.axis_index("rep") // 2]).astype(jnp.int32)
    rows, depth = hidden.shape
    k_rows, cols = x_weight.shape
    half = cols // 2
    heads = dt_bias.shape[0]
    mine = heads // 2
    map_cols = bc_weight.shape[1]
    used = map_cols + heads

    def shaped(dtype, *shape):
        return jax.ShapeDtypeStruct(shape, dtype)

    def at(p, l):
        return LANES * p + l

    swap = [(i, i ^ 1) for i in range(LANES * PLANES)]
    cores = [(i, i ^ 1) for i in range(lax.axis_size("rep"))]
    chips = [(i, i ^ 2) for i in range(lax.axis_size("rep"))]

    def shift(by, sources):
        return [(at(p, l), at(p + by, l)) for p in sources for l in range(LANES)]

    along = [(at(p, l), at((p + 1) % PLANES, l)) for p in range(PLANES) for l in range(LANES)]
    back = [(b, a) for a, b in along]

    def send(x, pairs, axis="seq"):
        return lax.ppermute(x, axis, pairs)

    together = lax.optimization_barrier

    ahead_at = (LANES * ((plane + 1) % PLANES) + core) * k_rows
    ahead = send(lax.dynamic_slice_in_dim(hidden, ahead_at, k_rows, 1), along)
    sent = lax.dynamic_slice_in_dim(x_weight, (1 - lane) * half, half, 1)
    other = send(sent, swap)
    own, small = call(
        split_kernel,
        [
            shaped(bf16, k_rows + used + heads, half),
            shaped(bf16, used + heads, k_rows),
        ],
        place,
        x_weight,
        bc_weight.T,
        dt_weight.T,
        seg_ids[None],
        left=4,
        grant=60,
        scratch=[
            pltpu.VMEM((heads, k_rows), bf16),
            pltpu.VMEM((1, rows), jnp.int32),
            pltpu.SemaphoreType.DMA((5,)),
        ],
    )
    own_one = send(own, along)
    small_next = send(small, back)
    near = pick(core == 0, hidden[:, : depth // 2], hidden[:, depth // 2 :])
    near, other = together((near, other))
    ahead_other = send(ahead, swap)
    other, own_one, ahead, ahead_other = together((other, own_one, ahead, ahead_other))

    other_one = send(other, along)
    own_two = send(own_one, along)
    near = send(near, swap)
    ahead = jnp.concatenate([ahead, ahead_other], axis=0)
    ahead_far = send(ahead, cores, "rep")
    part = call(
        neighbour_kernel,
        shaped(bf16, LANES * rows, half),
        place,
        ahead,
        ahead_far,
        own,
        other,
        flops=4 * rows * LANES * k_rows * half,
    )
    other_one, own_two, near, part = together((other_one, own_two, near, part))

    other_two = send(other_one, along)
    from_next = send(part, back)
    far = send(near, cores, "rep")
    share = call(
        functools.partial(share_kernel, used),
        shaped(f32, used + heads, LANES * rows),
        place,
        hidden,
        near,
        far,
        own,
        own_one,
        own_two,
        small_next,
        flops=4 * rows * depth * used,
        left=PLANES,
        scratch=[
            pltpu.VMEM((PLANES, used + heads, k_rows), bf16),
            pltpu.SemaphoreType.DMA((PLANES,)),
        ],
    )

    def early_products(backs, chunks, *totals):
        return call(
            functools.partial(early_kernel, backs),
            shaped(f32, LANES, rows, half),
            place,
            hidden,
            near,
            far,
            *totals,
            *chunks,
            flops=4 * rows * k_rows * half * len(backs),
        )

    early = early_products(
        ((0, True), (0, False), (1, True), (1, False)), (own, other, own_one, other_one)
    )
    early = early_products(((2, True),), (own_two,), early)
    share_other = send(share, swap)
    total = share + jnp.concatenate([share_other[:, rows:], share_other[:, :rows]], axis=1)
    some = total[:map_cols].astype(bf16)
    some_core = send(some, cores, "rep")
    some_chip = send(some, chips, "rep")
    some_both = send(some_chip, cores, "rep")
    mixing, loaded, c_rows, fac, meta, passing = call(
        functools.partial(decay_kernel, map_cols),
        [
            shaped(bf16, LANES, mine, rows, rows),
            shaped(bf16, LANES, mine, NS, rows),
            shaped(bf16, LANES, rows, NS),
            shaped(f32, LANES, rows, 8),
            shaped(f32, 8, half),
            shaped(bf16, 16, half),
        ],
        place,
        some,
        some_core,
        some_chip,
        some_both,
        total,
        dt_bias[:, None],
        decay_rate[:, None],
        flops=100 * mine * rows * rows,
    )
    inputs, ready, built = call(
        functools.partial(input_kernel, ((2, False),)),
        [
            shaped(bf16, LANES, rows, half),
            shaped(bf16, NS, half),
            shaped(bf16, NS, half),
        ],
        place,
        hidden,
        near,
        far,
        early,
        from_next,
        other_two,
        loaded,
        meta,
        flops=rows * depth * half,
    )
    passed = send(passing, shift(1, (0, 1, 2)))
    from_one = send(ready, shift(1, (0, 1, 2)))
    from_two = send(ready, shift(2, (0, 1)))
    local = call(
        local_kernel,
        shaped(f32, LANES, rows, half),
        place,
        inputs,
        mixing,
        skip[None],
        c_rows,
        built,
        fac,
        flops=4 * rows * rows * half,
    )

    def finish(partner):
        return call(
            functools.partial(final_kernel, partner, mine),
            shaped(bf16, rows, half),
            place,
            local,
            c_rows,
            fac,
            meta,
            passed,
            from_one,
            from_two,
            flops=2 * rows * NS * half,
        )

    swapped = send(finish(True), swap)
    kept = finish(False)
    return pick(
        even,
        jnp.concatenate([kept, swapped], axis=1),
        jnp.concatenate([swapped, kept], axis=1),
    )


def shards(hidden, seg_ids, x_weight, bc_weight, dt_weight, dt_bias, decay_rate, skip):
    heads = dt_bias.shape[0]
    by_planes = (
        lax.axis_size("seq") == LANES * PLANES
        and lax.axis_size("rep") == 4
        and heads == SUBLANES
        and 2 * x_weight.shape[0] == x_weight.shape[1] == heads * P_SIZE
        and 2 * bc_weight.shape[1] == NS
        and hidden.shape[0] <= x_weight.shape[0]
        and 2 * LANES * hidden.shape[0] >= DOC_MAX
    )
    plan = plane_shards if by_planes else gathered_shards
    return plan(hidden, seg_ids, x_weight, bc_weight, dt_weight, dt_bias, decay_rate, skip)


def solution(mesh):
    placed = (
        P("seq", None),
        P("seq"),
        P("seq", "rep"),
        P("seq", "rep"),
        P("seq", "rep"),
        P("rep"),
        P("rep"),
        P("rep"),
    )
    return jax.shard_map(
        shards,
        mesh=mesh,
        in_specs=placed,
        out_specs=P("seq", "rep"),
        check_vma=False,
    )
```

```python
import functools
import math

import jax
import jax.numpy as jnp
from jax import lax
from jax.experimental import pallas as pl
from jax.experimental.pallas import tpu as pltpu
from jax.sharding import PartitionSpec as P

P_SIZE = 128
NS = 128
DOC_MAX = 1024
LANES = 2
PLANES = 4
SUBLANES = 8


def passed_along(x, axis, by):
    peers = lax.axis_size(axis)
    pairs = [(i, i + by) for i in range(peers) if 0 <= i + by < peers]
    return lax.ppermute(x, axis, pairs)


def state_read(c_block, state):
    upper_part = state.astype(jnp.bfloat16)
    lower_part = (state - upper_part.astype(jnp.float32)).astype(jnp.bfloat16)
    first = jnp.einsum("tn,hnp->thp", c_block, upper_part, preferred_element_type=jnp.float32)
    second = jnp.einsum("tn,hnp->thp", c_block, lower_part, preferred_element_type=jnp.float32)
    return first + second


def block_step(state, prev_seg, x_block, b_block, c_block, dt_block, rate_block, seg_block):
    count = x_block.shape[0]
    cum = jnp.cumsum(rate_block, axis=0)
    order = jnp.arange(count)
    masked = (order[:, None] >= order[None, :]) & (seg_block[:, None] == seg_block[None, :])
    scores = jnp.dot(c_block, b_block.T, preferred_element_type=jnp.float32)
    cum_heads = cum.T
    gaps = cum_heads[:, :, None] - cum_heads[:, None, :]
    decay = jnp.where(masked[None], jnp.exp(jnp.where(masked[None], gaps, 0.0)), 0.0)
    mixing = (scores[None] * decay * dt_block.T[:, None, :]).astype(jnp.bfloat16)
    diag_part = jnp.einsum("htj,jhp->thp", mixing, x_block, preferred_element_type=jnp.float32)
    keep = (seg_block == prev_seg).astype(jnp.float32)
    factor = jnp.exp(cum) * keep[:, None]
    carried = state_read(c_block, state) * factor[:, :, None]
    last_seg = seg_block[count - 1]
    tail = (
        jnp.exp(cum[count - 1][None, :] - cum)
        * dt_block
        * (seg_block == last_seg).astype(jnp.float32)[:, None]
    )
    loaded = (tail.T[:, :, None] * b_block.astype(jnp.float32)[None]).astype(jnp.bfloat16)
    built = jnp.einsum("hjn,jhp->hnp", loaded, x_block, preferred_element_type=jnp.float32)
    through = jnp.exp(cum[count - 1]) * (last_seg == prev_seg).astype(jnp.float32)
    new_state = built + through[:, None, None] * state
    return (diag_part + carried, new_state, last_seg)


def combine(earlier, later):
    early_state, early_keep, early_first, early_last = earlier
    late_state, late_keep, late_first, late_last = later
    linked = ((early_last == late_first) | (early_last < 0) | (late_first < 0)).astype(jnp.float32)
    passing = late_keep * linked
    return (
        late_state + passing[:, None, None] * early_state,
        early_keep * passing,
        jnp.where(early_first < 0, late_first, early_first),
        jnp.where(late_last < 0, early_last, late_last),
    )


def gathered_shards(hidden, seg_ids, x_weight, bc_weight, dt_weight, dt_bias, decay_rate, skip):
    tok_rows = hidden.shape[0]
    heads = dt_bias.shape[0]
    width = x_weight.shape[1]
    x_rows, bc_rows, dt_rows = (
        lax.all_gather(x_weight, "seq", axis=0, tiled=True),
        lax.all_gather(bc_weight, "seq", axis=0, tiled=True),
        lax.all_gather(dt_weight, "seq", axis=0, tiled=True),
    )
    x_total = jnp.dot(hidden, x_rows, preferred_element_type=jnp.float32)
    bc_total = jnp.dot(hidden, bc_rows, preferred_element_type=jnp.float32)
    dt_total = jnp.dot(hidden, dt_rows, preferred_element_type=jnp.float32)
    inputs = x_total.astype(jnp.bfloat16).reshape(tok_rows, heads, P_SIZE)
    maps = lax.all_gather(bc_total.astype(jnp.bfloat16), "rep", axis=1, tiled=True)
    b_all = maps[:, :NS]
    c_all = maps[:, NS:]
    steps = jax.nn.softplus(dt_total + dt_bias)
    rates = -steps * decay_rate
    state = jnp.zeros((heads, NS, P_SIZE), jnp.float32)
    prev_seg = jnp.int32(-1)
    result, state, prev_seg = block_step(
        state, prev_seg, inputs, b_all, c_all, steps, rates, seg_ids
    )
    whole_keep = jnp.exp(jnp.sum(rates, axis=0)) * (seg_ids[0] == seg_ids[tok_rows - 1]).astype(
        jnp.float32
    )
    element = (state, whole_keep, seg_ids[:1], seg_ids[tok_rows - 1 :])
    reach = DOC_MAX // tok_rows + 1
    first_hop = passed_along((element[0], element[1], element[2], element[3]), "seq", 1)
    incoming = first_hop
    for hop in range(reach - 1):
        incoming = combine(
            passed_along((incoming[0], incoming[1], incoming[2], incoming[3]), "seq", 1), first_hop
        )
    state_in = incoming[0]
    tag_in = incoming[3]
    running = jnp.cumsum(rates, axis=0)
    factor = jnp.exp(running) * (seg_ids == tag_in[0]).astype(jnp.float32)[:, None]
    extra = state_read(c_all, state_in) * factor[:, :, None]
    total_out = result + extra + skip[None, :, None] * inputs.astype(jnp.float32)
    return total_out.astype(jnp.bfloat16).reshape(tok_rows, width)


def pick(first, one, other):
    return jnp.where(first, one, other)


def call(body, outs, *operands, flops=0, scratch=(), left=0, grant=16):
    single = not isinstance(outs, list)
    shapes = [outs] if single else outs
    size = sum(math.prod(o.shape) * o.dtype.itemsize for o in (*operands, *shapes))
    result = pl.pallas_call(
        body,
        out_shape=shapes,
        in_specs=[pl.BlockSpec(memory_space=pltpu.SMEM)]
        + [pl.BlockSpec(memory_space=pltpu.VMEM)] * (len(operands) - 1 - left)
        + [pl.BlockSpec(memory_space=pl.ANY)] * left,
        out_specs=[pl.BlockSpec(memory_space=pltpu.VMEM)] * len(shapes),
        scratch_shapes=list(scratch),
        compiler_params=pltpu.CompilerParams(vmem_limit_bytes=grant * 2**20),
        cost_estimate=pl.CostEstimate(flops=flops, bytes_accessed=size, transcendentals=0),
    )(*operands)
    return result[0] if single else result


def contract_last(a, b):
    return lax.dot_general(a, b, (((1,), (1,)), ((), ())), preferred_element_type=jnp.float32)


def mul(a, b):
    return jnp.dot(a, b, preferred_element_type=jnp.float32)


def depth_blocks(place, token_refs, at, size):
    hidden_ref, near_ref, far_ref = token_refs
    own = hidden_ref[:, pl.ds(pl.multiple_of(at * size, size), size)]
    blocks = near_ref.shape[1] // size
    inside = pl.ds(pl.multiple_of((at % blocks) * size, size), size)
    is_near = (at // blocks) == place[2]
    return own, jnp.where(is_near, near_ref[:, inside], far_ref[:, inside])


def split_kernel(place, x_weight, bc, dt, ids, own, small, below, ids_in, done):
    f32, bf16 = jnp.float32, jnp.bfloat16
    lane = place[1]
    size, half = x_weight.shape[0], x_weight.shape[1] // 2
    maps, heads, rows = bc.shape[0], dt.shape[0], ids.shape[1]
    def columns(ref, index, width):
        return ref.at[:, pl.ds(pl.multiple_of(index * width, width), width)]

    moves = [
        (columns(x_weight, lane, half), own.at[pl.ds(0, size), :]),
        (bc, own.at[pl.ds(size, maps), :]),
        (bc, small.at[pl.ds(0, maps), :]),
        (dt, below),
        (ids, ids_in),
    ]
    copies = [pltpu.make_async_copy(a, b, done.at[i]) for i, (a, b) in enumerate(moves)]
    for copy in copies:
        copy.start()
    for copy in copies:
        copy.wait()
    row = lax.broadcasted_iota(jnp.int32, (heads, rows), 0)
    notes = jnp.where(row == 0, ids_in[...].astype(f32), 0.0)
    notes = jnp.concatenate([notes, jnp.zeros((heads, size - rows), f32)], axis=1)
    last = jnp.concatenate([below[...].astype(f32), notes], axis=0).astype(bf16)
    own[size + maps :, :] = last
    small[maps:, :] = last


def share_kernel(used, place, hidden, near, far, c0, c1, c2, s3, out):
    plane, lane = place[0], place[1]
    rows = hidden.shape[0]
    size = c0.shape[1]
    totals = [None, None]
    for back, s in enumerate((c0, c1, c2, s3)):
        at = LANES * ((plane + PLANES - back) % PLANES) + lane
        weights = s[...]
        for r, tokens in enumerate(depth_blocks(place, (hidden, near, far), at, size)):
            product = contract_last(weights, tokens)
            totals[r] = product if totals[r] is None else totals[r] + product
    notes = [s[used:, :rows].astype(jnp.float32) for s in (c0, c1, c2)]
    row = lax.broadcasted_iota(jnp.int32, notes[0].shape, 0)
    ends = [n[0:1, rows - 1 : rows] for n in notes[1:]]
    note = jnp.where(row == 1, ends[0], jnp.where(row == 2, ends[1], notes[0]))
    out[:used, :rows] = totals[0][:used]
    out[:used, rows:] = totals[1][:used]
    out[used:, :rows] = note
    out[used:, rows:] = jnp.zeros_like(note)


def decay_kernel(
    map_cols, place, some, some_core, some_chip, some_both, total, bias, rate_of, mixing, loaded, c_out, fac, meta, passing
):
    f32, bf16 = jnp.float32, jnp.bfloat16
    plane, lane = place[0], place[1]
    first_core, first_chip = place[2] == 0, place[3] == 0
    here = [pick(first_core, a[...], b[...]) for a, b in ((some, some_core), (some_core, some))]
    there = [
        pick(first_core, a[...], b[...])
        for a, b in ((some_chip, some_both), (some_both, some_chip))
    ]
    here, there = jnp.concatenate(here, axis=0), jnp.concatenate(there, axis=0)
    b_maps, c_maps = pick(first_chip, here, there), pick(first_chip, there, here)
    heads = bias.shape[0]
    mine = heads // 2
    rows = total.shape[1] // 2
    even = lane == 0
    pre = total[map_cols : map_cols + heads, :] + bias[...]
    steps = jnp.maximum(pre, 0.0) + jnp.log1p(jnp.exp(-jnp.abs(pre)))
    rates = -steps * rate_of[...]
    steps = jnp.where(even, steps[:mine], steps[mine:])
    rates = jnp.where(even, rates[:mine], rates[mine:])
    notes = total[map_cols + heads :, :]
    tri_row = lax.broadcasted_iota(jnp.int32, (rows, rows), 0)
    tri_col = lax.broadcasted_iota(jnp.int32, (rows, rows), 1)
    upper = (tri_row <= tri_col).astype(f32)
    causal = tri_row >= tri_col
    pad = jnp.zeros((8 - mine, rows), f32)
    cums, lasts = [], []
    for r in range(2):
        cut = slice(r * rows, (r + 1) * rows)
        cums.append(
            lax.dot_general(
                jnp.concatenate([rates[:, cut], pad], axis=0),
                upper,
                (((1,), (0,)), ((), ())),
                precision=lax.Precision.HIGHEST,
                preferred_element_type=f32,
            )
        )
        lasts.append(notes[0:1, (r + 1) * rows - 1 : (r + 1) * rows])
    end = [c[:mine, rows - 1 : rows] for c in cums]
    end0, end1 = pick(even, end[0], end[1]), pick(even, end[1], end[0])
    last0, last1 = pick(even, lasts[0], lasts[1]), pick(even, lasts[1], lasts[0])
    final = pick(even, notes[:, 2 * rows - 1 :], notes[:, rows - 1 : rows])
    tag = jnp.where(plane > 0, final[1:2], -1.0)
    tag_before = jnp.where(plane > 1, final[2:3], -1.0)
    link = jnp.exp(end1) * (last1 == last0).astype(f32)
    enters = jnp.exp(end0) * (last0 == tag).astype(f32)
    through = jnp.exp(end0 + end1)
    passes = (tag == tag_before).astype(f32)
    width = meta.shape[1] // mine
    meta[...] = jnp.zeros_like(meta)
    for h in range(mine):
        cut = slice(h * width, (h + 1) * width)
        meta[0:1, cut] = jnp.broadcast_to(link[h : h + 1], (1, width))
        meta[1:2, cut] = jnp.broadcast_to(enters[h : h + 1], (1, width))
        meta[2:3, cut] = jnp.broadcast_to(through[h : h + 1], (1, width))
        meta[3:4, cut] = jnp.broadcast_to(passes, (1, width))
    whole = meta[2:3, :]
    upper_part = whole.astype(bf16).astype(f32)
    row = lax.broadcasted_iota(jnp.int32, passing.shape, 0)
    passing[...] = jnp.where(
        row == 0, upper_part, jnp.where(row == 1, whole - upper_part, 0.0)
    ).astype(bf16)
    for r in range(2):
        b = lane if r == 0 else 1 - lane
        cut = slice(r * rows, (r + 1) * rows)
        seg, cum, dt = notes[0:1, cut], cums[r], steps[:, cut]
        source = jnp.where(b == 0, tag, last0)
        factor = jnp.exp(cum) * (seg == source).astype(f32)
        fac[b] = factor.T
        cols = jnp.concatenate([cum[:mine], jnp.broadcast_to(seg, (8 - mine, rows))], axis=0).T
        keep = causal & (cols[:, mine : mine + 1] == seg)
        b_t, c_t = b_maps[:, cut], c_maps[:, cut]
        c_rows = c_t.astype(f32).T.astype(bf16)
        c_out[b] = c_rows
        scores = mul(c_rows, b_t)
        tail = jnp.exp(end[r] - cum[:mine]) * dt * (seg == lasts[r]).astype(f32)
        wide = b_t.astype(f32)
        for h in range(mine):
            gap = cols[:, h : h + 1] - cum[h : h + 1]
            decay = jnp.where(keep, jnp.exp(jnp.where(keep, gap, 0.0)), 0.0)
            mixing[b, h] = (scores * decay * dt[h : h + 1]).astype(bf16)
            loaded[b, h] = (wide * tail[h : h + 1]).astype(bf16)


def add_products(place, token_refs, backs, weight_refs, totals):
    plane, lane = place[0], place[1]
    for (back, is_own), w in zip(backs, weight_refs):
        at = LANES * ((plane + PLANES - back) % PLANES) + (lane if is_own else 1 - lane)
        size = w.shape[1]
        weights = w[:size, :]
        for r, tokens in enumerate(depth_blocks(place, token_refs, at, size)):
            product = mul(tokens, weights)
            totals[r] = product if totals[r] is None else totals[r] + product


def early_kernel(backs, place, hidden, near, far, *refs):
    *weights, out = refs
    totals = [None, None]
    if len(weights) > len(backs):
        totals = [weights[0][0], weights[0][1]]
        weights = weights[1:]
    add_products(place, (hidden, near, far), backs, weights, totals)
    out[0] = totals[0]
    out[1] = totals[1]


def neighbour_kernel(place, mine, far, own, other, out):
    same = place[1] == place[2]
    size = other.shape[0]
    here, there = mine[...], far[...]
    first, second = jnp.where(same, here, there), jnp.where(same, there, here)
    out[...] = (mul(first, own[:size, :]) + mul(second, other[...])).astype(out.dtype)


def input_kernel(backs, place, hidden, near, far, acc, back, *refs):
    *chunks, loaded, meta, x_out, ready, built_out = refs
    f32, bf16 = jnp.float32, jnp.bfloat16
    lane = place[1]
    rows = hidden.shape[0]
    totals = [acc[0] + back[:rows, :].astype(f32), acc[1] + back[rows : 2 * rows, :].astype(f32)]
    add_products(place, (hidden, near, far), backs, chunks, totals)
    x_out[lane] = totals[0].astype(bf16)
    x_out[1 - lane] = totals[1].astype(bf16)
    mine = loaded.shape[1]
    width = meta.shape[1] // mine
    for h in range(mine):
        cut = slice(h * width, (h + 1) * width)
        first = mul(loaded[0, h], x_out[0, :, cut])
        second = mul(loaded[1, h], x_out[1, :, cut])
        ready[:, cut] = (second + meta[0:1, cut] * first).astype(bf16)
        built_out[:, cut] = first.astype(bf16)


def local_kernel(place, x, mixing, skip, c_rows, built, fac, out):
    lane = place[1]
    mine = mixing.shape[1]
    width = x.shape[2] // mine
    carried = mul(c_rows[1], built[...])
    gains = jnp.where(lane == 0, skip[:, :mine], skip[:, mine:])
    for h in range(mine):
        cut = slice(h * width, (h + 1) * width)
        for b in range(2):
            xs = x[b, :, cut]
            local = mul(mixing[b, h], xs) + gains[:, h : h + 1] * xs.astype(jnp.float32)
            if b == 1:
                local = local + fac[1, :, h : h + 1] * carried[:, cut]
            out[b, :, cut] = local


def final_kernel(partner, mine, place, local, c_rows, fac, meta, passed, one, two, out):
    f32, bf16 = jnp.float32, jnp.bfloat16
    lane = place[1]
    b = 1 - lane if partner else lane
    through = passed[0:1, :].astype(f32) + passed[1:2, :].astype(f32)
    incoming = one[...].astype(f32) + (through * meta[3:4, :]) * two[...].astype(f32)
    entering = (incoming * jnp.where(b == 1, meta[1:2, :], 1.0)).astype(bf16)
    carried = mul(c_rows[b], entering)
    factor = fac[b]
    width = out.shape[1] // mine
    for h in range(mine):
        cut = slice(h * width, (h + 1) * width)
        out[:, cut] = (local[b, :, cut] + factor[:, h : h + 1] * carried[:, cut]).astype(bf16)


def plane_shards(hidden, seg_ids, x_weight, bc_weight, dt_weight, dt_bias, decay_rate, skip):
    bf16, f32 = jnp.bfloat16, jnp.float32
    me = lax.axis_index("seq")
    lane, plane = me % LANES, me // LANES
    even = lane == 0
    core = lax.axis_index("rep") % 2
    place = jnp.stack([plane, lane, core, lax.axis_index("rep") // 2]).astype(jnp.int32)
    rows, depth = hidden.shape
    k_rows, cols = x_weight.shape
    half = cols // 2
    heads = dt_bias.shape[0]
    mine = heads // 2
    map_cols = bc_weight.shape[1]
    used = map_cols + heads

    def shaped(dtype, *shape):
        return jax.ShapeDtypeStruct(shape, dtype)

    def at(p, l):
        return LANES * p + l

    swap = [(i, i ^ 1) for i in range(LANES * PLANES)]
    cores = [(i, i ^ 1) for i in range(lax.axis_size("rep"))]
    chips = [(i, i ^ 2) for i in range(lax.axis_size("rep"))]

    def shift(by, sources):
        return [(at(p, l), at(p + by, l)) for p in sources for l in range(LANES)]

    along = [(at(p, l), at((p + 1) % PLANES, l)) for p in range(PLANES) for l in range(LANES)]
    back = [(b, a) for a, b in along]

    def send(x, pairs, axis="seq"):
        return lax.ppermute(x, axis, pairs)

    together = lax.optimization_barrier

    ahead_at = (LANES * ((plane + 1) % PLANES) + core) * k_rows
    ahead = send(lax.dynamic_slice_in_dim(hidden, ahead_at, k_rows, 1), along)
    sent = lax.dynamic_slice_in_dim(x_weight, (1 - lane) * half, half, 1)
    other = send(sent, swap)
    own, small = call(
        split_kernel,
        [
            shaped(bf16, k_rows + used + heads, half),
            shaped(bf16, used + heads, k_rows),
        ],
        place,
        x_weight,
        bc_weight.T,
        dt_weight.T,
        seg_ids[None],
        left=4,
        grant=60,
        scratch=[
            pltpu.VMEM((heads, k_rows), bf16),
            pltpu.VMEM((1, rows), jnp.int32),
            pltpu.SemaphoreType.DMA((5,)),
        ],
    )
    own_one = send(own, along)
    small_next = send(small, back)
    near = pick(core == 0, hidden[:, : depth // 2], hidden[:, depth // 2 :])
    near, other = together((near, other))
    ahead_other = send(ahead, swap)
    other, own_one, ahead, ahead_other = together((other, own_one, ahead, ahead_other))

    other_one = send(other, along)
    own_two = send(own_one, along)
    near = send(near, swap)
    ahead = jnp.concatenate([ahead, ahead_other], axis=0)
    ahead_far = send(ahead, cores, "rep")
    part = call(
        neighbour_kernel,
        shaped(bf16, LANES * rows, half),
        place,
        ahead,
        ahead_far,
        own,
        other,
        flops=4 * rows * LANES * k_rows * half,
    )
    below_one = own_one[k_rows:]
    other_one, own_two, near, part, below_one = together(
        (other_one, own_two, near, part, below_one)
    )

    other_two = send(other_one, along)
    from_next = send(part, back)
    far = send(near, cores, "rep")
    share = call(
        functools.partial(share_kernel, used),
        shaped(f32, used + heads, LANES * rows),
        place,
        hidden,
        near,
        far,
        small,
        below_one,
        own_two[k_rows:],
        small_next,
        flops=4 * rows * depth * used,
    )

    def early_products(backs, chunks, *totals):
        return call(
            functools.partial(early_kernel, backs),
            shaped(f32, LANES, rows, half),
            place,
            hidden,
            near,
            far,
            *totals,
            *chunks,
            flops=4 * rows * k_rows * half * len(backs),
        )

    early = early_products(
        ((0, True), (0, False), (1, True), (1, False)), (own, other, own_one, other_one)
    )
    early = early_products(((2, True),), (own_two,), early)
    share_other = send(share, swap)
    total = share + jnp.concatenate([share_other[:, rows:], share_other[:, :rows]], axis=1)
    some = total[:map_cols].astype(bf16)
    some_core = send(some, cores, "rep")
    some_chip = send(some, chips, "rep")
    some_both = send(some_chip, cores, "rep")
    mixing, loaded, c_rows, fac, meta, passing = call(
        functools.partial(decay_kernel, map_cols),
        [
            shaped(bf16, LANES, mine, rows, rows),
            shaped(bf16, LANES, mine, NS, rows),
            shaped(bf16, LANES, rows, NS),
            shaped(f32, LANES, rows, 8),
            shaped(f32, 8, half),
            shaped(bf16, 16, half),
        ],
        place,
        some,
        some_core,
        some_chip,
        some_both,
        total,
        dt_bias[:, None],
        decay_rate[:, None],
        flops=100 * mine * rows * rows,
    )
    inputs, ready, built = call(
        functools.partial(input_kernel, ((2, False),)),
        [
            shaped(bf16, LANES, rows, half),
            shaped(bf16, NS, half),
            shaped(bf16, NS, half),
        ],
        place,
        hidden,
        near,
        far,
        early,
        from_next,
        other_two,
        loaded,
        meta,
        flops=rows * depth * half,
    )
    passed = send(passing, shift(1, (0, 1, 2)))
    from_one = send(ready, shift(1, (0, 1, 2)))
    from_two = send(ready, shift(2, (0, 1)))
    local = call(
        local_kernel,
        shaped(f32, LANES, rows, half),
        place,
        inputs,
        mixing,
        skip[None],
        c_rows,
        built,
        fac,
        flops=4 * rows * rows * half,
    )

    def finish(partner):
        return call(
            functools.partial(final_kernel, partner, mine),
            shaped(bf16, rows, half),
            place,
            local,
            c_rows,
            fac,
            meta,
            passed,
            from_one,
            from_two,
            flops=2 * rows * NS * half,
        )

    swapped = send(finish(True), swap)
    kept = finish(False)
    return pick(
        even,
        jnp.concatenate([kept, swapped], axis=1),
        jnp.concatenate([swapped, kept], axis=1),
    )


def shards(hidden, seg_ids, x_weight, bc_weight, dt_weight, dt_bias, decay_rate, skip):
    heads = dt_bias.shape[0]
    by_planes = (
        lax.axis_size("seq") == LANES * PLANES
        and lax.axis_size("rep") == 4
        and heads == SUBLANES
        and 2 * x_weight.shape[0] == x_weight.shape[1] == heads * P_SIZE
        and 2 * bc_weight.shape[1] == NS
        and hidden.shape[0] <= x_weight.shape[0]
        and 2 * LANES * hidden.shape[0] >= DOC_MAX
    )
    plan = plane_shards if by_planes else gathered_shards
    return plan(hidden, seg_ids, x_weight, bc_weight, dt_weight, dt_bias, decay_rate, skip)


def solution(mesh):
    placed = (
        P("seq", None),
        P("seq"),
        P("seq", "rep"),
        P("seq", "rep"),
        P("seq", "rep"),
        P("rep"),
        P("rep"),
        P("rep"),
    )
    return jax.shard_map(
        shards,
        mesh=mesh,
        in_specs=placed,
        out_specs=P("seq", "rep"),
        check_vma=False,
    )
```
